32 devices in a mesh: row: 8 (over y, x, core), col: 4 (over z).
Axes of the slice: x: 2, y: 2, z: 4, core: 2. Of those that a mesh axis runs over, the one named last changes fastest.
Arguments:
- inputs: bfloat16 [8192, 2048], P('row', 'col'), may hold values from -6 to 6
- cotangent: bfloat16 [8192, 2048], P('row', 'col'), may hold values from -6 to 6
- attention_norm_gain: float32 [2048], replicated, may hold values from 0.28 to 2.6
- expert_norm_gain: float32 [2048], replicated, may hold values from 0.5 to 1.5
- query_norm_gain: float32 [128], replicated, may hold values from 0.5 to 1.5
- key_norm_gain: float32 [128], replicated, may hold values from 0.5 to 1.5
- frozen_query_weight: bfloat16 [2048, 4096], P('row', 'col'), may hold values from -0.125 to 0.125
- frozen_key_weight: bfloat16 [2048, 512], P('row'), may hold values from -0.125 to 0.125
- frozen_value_weight: bfloat16 [2048, 512], P('row'), may hold values from -0.125 to 0.125
- frozen_output_weight: bfloat16 [4096, 2048], P('col', 'row'), may hold values from -1.5 to 1.5
- frozen_router_weight: bfloat16 [2048, 16], P('row'), may hold values from -0.0625 to 0.0625
- expert_gate_up_weight: bfloat16 [16, 2048, 1536], P('col', 'row'), may hold values from -0.125 to 0.125
- expert_down_weight: bfloat16 [16, 768, 2048], P('col', None, 'row'), may hold values from -1.25 to 1.25
- adapter_input_down: float32 [8, 2048, 48], P(None, 'row'), may hold values from -0.125 to 0.125
- adapter_query_up: float32 [8, 16, 4096], P(None, None, 'col'), may hold values from -0.75 to 0.75
- adapter_key_value_up: float32 [8, 2, 16, 512], replicated, may hold values from -0.75 to 0.75
- adapter_output_down: float32 [8, 4096, 16], P(None, 'col'), may hold values from -1.5 to 1.5
- adapter_output_up: float32 [8, 2048, 16], P(None, 'row'), may hold values from -0.75 to 0.75
- input_first_moment: float32 [8, 2048, 48], P(None, 'row'), may hold values from -0.0004272461 to 0.0004272461
- input_second_moment: float32 [8, 2048, 48], P(None, 'row'), may hold values from 4.4878792e-10 to 1.7951517e-09
- query_first_moment: float32 [8, 16, 4096], P(None, None, 'col'), may hold values from -7.6293945e-05 to 7.6293945e-05
- query_second_moment: float32 [8, 16, 4096], P(None, None, 'col'), may hold values from 1.3463637e-11 to 5.385455e-11
- key_value_first_moment: float32 [8, 2, 16, 512], replicated, may hold values from -0.0004272461 to 0.0004272461
- key_value_second_moment: float32 [8, 2, 16, 512], replicated, may hold values from 4.4878792e-10 to 1.7951517e-09
- output_down_first_moment: float32 [8, 4096, 16], P(None, 'col'), may hold values from -4.5776367e-05 to 4.5776367e-05
- output_down_second_moment: float32 [8, 4096, 16], P(None, 'col'), may hold values from 4.4878793e-12 to 1.7951517e-11
- output_up_first_moment: float32 [8, 2048, 16], P(None, 'row'), may hold values from -9.1552734e-05 to 9.1552734e-05
- output_up_second_moment: float32 [8, 2048, 16], P(None, 'row'), may hold values from 1.7951517e-11 to 7.180607e-11
- routes: int32 [8192, 8], P('row'), may hold values from 0 to 15, all different within a row; in each aligned block of 1024 rows (0 to 1023, 1024 to 2047, ...) at most 1024 rows name the same one
- tree_adapter_index: int32 [8], P('row'), may hold values from 0 to 7
- tree_node_length: int32 [8, 13], P('row'), may hold values from 1 to 512, 1024 in all within a row
- parents: int32 [8, 13], P('row'), may hold values from 0 to 4, as said below
Outputs:
- layer_output: float32 [8192, 2048], P('row', 'col')
- input_grad: float32 [8192, 2048], P('row', 'col')
- grad_norm: float32 [], replicated
- lora_in_next: float32 [8, 2048, 48], P(None, 'row')
- first_in_next: float32 [8, 2048, 48], P(None, 'row')
- second_in_next: float32 [8, 2048, 48], P(None, 'row')
- lora_query_next: float32 [8, 16, 4096], P(None, None, 'col')
- first_query_next: float32 [8, 16, 4096], P(None, None, 'col')
- second_query_next: float32 [8, 16, 4096], P(None, None, 'col')
- lora_kv_next: float32 [8, 2, 16, 512], replicated
- first_kv_next: float32 [8, 2, 16, 512], replicated
- second_kv_next: float32 [8, 2, 16, 512], replicated
- lora_out_down_next: float32 [8, 4096, 16], P(None, 'col')
- first_out_down_next: float32 [8, 4096, 16], P(None, 'col')
- second_out_down_next: float32 [8, 4096, 16], P(None, 'col')
- lora_out_up_next: float32 [8, 2048, 16], P(None, 'row')
- first_out_up_next: float32 [8, 2048, 16], P(None, 'row')
- second_out_up_next: float32 [8, 2048, 16], P(None, 'row')
- expert_output: float32 [8192, 2048], P('row', 'col')
The draws below stay inside these ranges and needn't reach their ends.
Inputs may be any that keep to these rules, and one draw needn't show every extreme that they name: `parents`: node 0 is the trunk and its own parent; nodes 1 to 4 hang from node 0; every later node hangs from one of nodes 1 to 4. `routes`: no expert is named by more than 1024 rows of one tree.
All inputs are finite; a program needn't handle non-finite values.
Results may differ from the reference program's by a relative error of at most 0.025.
Values may be sent and summed in bfloat16 or wider, within the bound.
No kernel may reach another device: no remote copies, remote signals or barrier semaphores. Data moves between devices by JAX's collectives and lax.ppermute only.
A program may use at most 384 MiB of HBM per device.

```python
import math
import jax
import jax.numpy as jnp
import numpy as np
from jax import lax

MODEL_WIDTH = 2048
QUERY_HEADS = 32
KEY_VALUE_HEADS = 4
HEAD_WIDTH = 128
F = 768
TOP = 8
ADAPTER_RANK = 16
ADAPTER_TOTAL = 8
NODES = 13
STEP = 10
TOK_DEV = 1024
EXPERTS = 16
TREES = 8
TOKENS = 8192
CAP = 1024
NPARAM = 2228224


def draw_attention_norm_gain(key, part):
    key = jax.random.fold_in(key, 7)
    ramp = jnp.arange(MODEL_WIDTH, dtype=jnp.float32) / MODEL_WIDTH
    base = 0.5 + ramp
    noise = jax.random.uniform(key, (MODEL_WIDTH,), jnp.float32, 0.8, 1.2)
    return base * noise


def draw_parents(key, part):
    key = jax.random.fold_in(key, 11)
    leaves = jax.random.randint(key, (TREES, NODES - 5), 1, 5, dtype=jnp.int32)
    trunk_branch = jnp.zeros((TREES, 5), jnp.int32)
    return jnp.concatenate([trunk_branch, leaves], axis=1)


def with_ends(result, rng, least, top_value):
    spot = [jax.random.randint(jax.random.fold_in(rng, axis), (), 0, length) for axis, length in enumerate(result.shape)]
    widest = result.shape.index(max(result.shape))
    neighbour = spot[:widest] + [(spot[widest] + 1) % result.shape[widest]] + spot[widest + 1:]
    return result.at[tuple(spot)].set(least).at[tuple(neighbour)].set(top_value)


def levels(key, dims, shards, least, largest):
    def one(dim, blocks):
        steps = jax.random.uniform(jax.random.fold_in(jax.random.fold_in(key, 6), dim), (blocks,), jnp.float32, least / len(shards), largest / len(shards))
        return jnp.repeat(jnp.exp(steps), dims[dim] // blocks).reshape((-1,) + (1,) * (len(dims) - dim - 1))

    factor_of = one(*shards[0])
    for cut in shards[1:]:
        factor_of = factor_of * one(*cut)
    return factor_of


def length_profile(count, total, reach, skew):
    portions = [(1 << 20) // math.isqrt(rank ** skew) + 1 for rank in range(2, count + 1)]
    spare, counts = total - reach - (count - 1), [1] * (count - 1)
    while spare > 0:
        free = [i for i in range(count - 1) if counts[i] < reach]
        mass, budget = sum([portions[i] for i in free]), spare
        for i in free:
            extra = min(reach - counts[i], max(1, budget * portions[i] // mass), spare)
            counts[i] = counts[i] + extra
            spare = spare - extra
    return np.array([reach] + counts)


def ragged_sizes(stream_key, count, total, most, lean):
    if count == 2:
        one = jax.random.randint(stream_key, (), max(1, total - most), min(most, total - 1) + 1)
        return jnp.stack([one, total - one])
    tallies = jnp.asarray(length_profile(count, total, most, lean), jnp.int32)
    couples = (count - 1) // 2
    giver, sink = tallies[1:1 + 2 * couples:2], tallies[2:2 + 2 * couples:2]
    room = jnp.minimum(giver - 1, most - sink)
    moved = jax.random.randint(jax.random.fold_in(stream_key, 1), (couples,), 0, 1 << 20) % (room + 1)
    tallies = tallies.at[1:1 + 2 * couples:2].set(giver - moved).at[2:2 + 2 * couples:2].set(sink + moved)
    return tallies[jax.random.permutation(jax.random.fold_in(stream_key, 2), count)]


def assign_block(key, own, number, rows, amount, top, most, slope):
    order = jax.random.permutation(key, amount)
    crowded, usual = portions_of(amount, rows * top, most, slope, True), portions_of(amount, rows * top, most, slope, False)
    places = jnp.arange(amount)

    def named(sizes, rotation):
        used = int((sizes > 0).sum())
        fixed = max(1, used // 4)
        shifted = fixed + (places - fixed + rotation * (used - fixed)) % max(1, amount - fixed)
        return jnp.zeros((amount,), jnp.int32).at[order[jnp.where(places < fixed, places, shifted)]].set(jnp.asarray(sizes, jnp.int32))

    sizes = jnp.where(number % 4 == 0, named(crowded, number // 4), named(usual, number - number // 4 - 1))
    mixed = jax.random.permutation(jax.random.fold_in(own, 3), amount)
    giver, receiver = mixed[0:amount // 2 * 2:2], mixed[1:amount // 2 * 2:2]
    margin = jnp.minimum(sizes[giver] - 1, most - sizes[receiver]) // 2
    margin = jnp.where((giver == order[0]) | (receiver == order[0]) | (sizes[receiver] == 0), 0, jnp.maximum(margin, 0))
    shifted = jax.random.randint(jax.random.fold_in(own, 4), (amount // 2,), 0, 1 << 20) % (margin + 1)
    sizes = sizes.at[giver].add(-shifted).at[receiver].add(shifted)
    labels = jnp.searchsorted(jnp.cumsum(sizes), jnp.arange(rows * top), side="right").astype(jnp.int32)
    table = labels.reshape(top, rows).T
    table = table[jax.random.permutation(jax.random.fold_in(own, 1), rows)]
    rotation = jax.random.randint(jax.random.fold_in(own, 2), (rows, 1), 0, top)
    return jnp.take_along_axis(table, (jnp.arange(top)[None, :] + rotation) % top, axis=1)


def portions_of(number_of, total, limit, skew, full):
    loads = [(1 << 20) // math.isqrt(grade ** skew) + 1 for grade in range(1, number_of + 1)]
    largest = limit if full else min(limit, max(-(-total // number_of), total * loads[0] // sum(loads)))
    least = 1 if total - largest >= number_of - 1 else 0
    holding, rest = [largest] + [least] * (number_of - 1), total - largest - least * (number_of - 1)
    while rest > 0:
        candidates = [i for i in range(1, number_of) if holding[i] < largest] or [i for i in range(1, number_of) if holding[i] < limit]
        pool, left = sum([loads[i] for i in candidates]), rest
        for i in candidates:
            addition = min(limit - holding[i], max(1, left * loads[i] // pool), rest)
            holding[i] = holding[i] + addition
            rest = rest - addition
    return np.array(holding)


def scatter_about(key, dims, scale, reach, cuts=(), kind=jnp.bfloat16):
    level = levels(key, dims, cuts, -0.22, 0.18) if cuts else 1.0
    values = jax.random.normal(key, dims, jnp.float32) * scale * level
    return jnp.minimum(jnp.maximum(values, -reach), reach).astype(kind)


def setup_inputs(seed: int = 0) -> dict:
    key_list = jax.random.split(jax.random.key(seed), 33)
    inputs = scatter_about(key_list[0], (TOKENS, MODEL_WIDTH), 1.0, 6.0, ((0, 8), (1, 4)))
    cotangent = scatter_about(key_list[1], (TOKENS, MODEL_WIDTH), 1.0, 6.0, ((0, 8), (1, 4)))
    attention_norm_gain = draw_attention_norm_gain(jax.random.fold_in(key_list[32], 71), 0)
    expert_norm_gain = jnp.clip(1.0 + 0.1 * jax.random.normal(key_list[3], (MODEL_WIDTH,), jnp.float32), 0.5, 1.5)
    query_norm_gain = jnp.clip(1.0 + 0.1 * jax.random.normal(key_list[4], (HEAD_WIDTH,), jnp.float32), 0.5, 1.5)
    key_norm_gain = jnp.clip(1.0 + 0.1 * jax.random.normal(key_list[5], (HEAD_WIDTH,), jnp.float32), 0.5, 1.5)
    frozen_query_weight = scatter_about(key_list[6], (MODEL_WIDTH, QUERY_HEADS * HEAD_WIDTH), MODEL_WIDTH ** -0.5, 0.125, ((0, 8), (1, 4)))
    frozen_key_weight = scatter_about(key_list[7], (MODEL_WIDTH, KEY_VALUE_HEADS * HEAD_WIDTH), MODEL_WIDTH ** -0.5, 0.125, ((0, 8),))
    frozen_value_weight = scatter_about(key_list[8], (MODEL_WIDTH, KEY_VALUE_HEADS * HEAD_WIDTH), MODEL_WIDTH ** -0.5, 0.125, ((0, 8),))
    frozen_output_weight = scatter_about(key_list[9], (QUERY_HEADS * HEAD_WIDTH, MODEL_WIDTH), (max(QUERY_HEADS * HEAD_WIDTH // 256, 4)) ** -0.5, 1.5, ((0, 4), (1, 8)))
    frozen_router_weight = scatter_about(key_list[10], (MODEL_WIDTH, EXPERTS), (0.5 / MODEL_WIDTH ** 0.5), 0.0625, ((0, 8),))
    expert_gate_up_weight = scatter_about(key_list[11], (EXPERTS, MODEL_WIDTH, 2 * F), MODEL_WIDTH ** -0.5, 0.125, ((0, 4), (1, 8)))
    expert_down_weight = scatter_about(key_list[12], (EXPERTS, F, MODEL_WIDTH), (F // 32) ** -0.5, 1.25, ((0, 4), (2, 8)))
    adapter_input_down = scatter_about(key_list[13], (ADAPTER_TOTAL, MODEL_WIDTH, 3 * ADAPTER_RANK), MODEL_WIDTH ** -0.5, 0.125, ((1, 8),), jnp.float32)
    adapter_query_up = scatter_about(key_list[14], (ADAPTER_TOTAL, ADAPTER_RANK, QUERY_HEADS * HEAD_WIDTH), (4 * ADAPTER_RANK) ** -0.5, 0.75, ((2, 4),), jnp.float32)
    adapter_key_value_up = scatter_about(key_list[15], (ADAPTER_TOTAL, 2, ADAPTER_RANK, KEY_VALUE_HEADS * HEAD_WIDTH), (4 * ADAPTER_RANK) ** -0.5, 0.75, (), jnp.float32)
    adapter_output_down = scatter_about(key_list[16], (ADAPTER_TOTAL, QUERY_HEADS * HEAD_WIDTH, ADAPTER_RANK), (max(QUERY_HEADS * HEAD_WIDTH // 256, 4)) ** -0.5, 1.5, ((1, 4),), jnp.float32)
    adapter_output_up = scatter_about(key_list[17], (ADAPTER_TOTAL, MODEL_WIDTH, ADAPTER_RANK), (4 * ADAPTER_RANK) ** -0.5, 0.75, ((1, 8),), jnp.float32)
    input_first_moment = scatter_about(key_list[18], (ADAPTER_TOTAL, MODEL_WIDTH, 3 * ADAPTER_RANK), (0.11 / NPARAM ** 0.5), 0.0004272461, ((1, 8),), jnp.float32)
    input_second_moment = jnp.clip(jnp.exp(math.log(1.7951516939618273e-09) - 1.3862944 * jax.random.uniform(key_list[19], (ADAPTER_TOTAL, MODEL_WIDTH, 3 * ADAPTER_RANK), jnp.float32) ** levels(key_list[19], (ADAPTER_TOTAL, MODEL_WIDTH, 3 * ADAPTER_RANK), ((1, 8),), -0.2, 0.2)), 4.487879234904568e-10, 1.7951516939618273e-09)
    query_first_moment = scatter_about(key_list[20], (ADAPTER_TOTAL, ADAPTER_RANK, QUERY_HEADS * HEAD_WIDTH), (0.02 / NPARAM ** 0.5), 7.62939453125e-05, ((2, 4),), jnp.float32)
    query_second_moment = jnp.clip(jnp.exp(math.log(5.385454929229816e-11) - 1.3862944 * jax.random.uniform(key_list[21], (ADAPTER_TOTAL, ADAPTER_RANK, QUERY_HEADS * HEAD_WIDTH), jnp.float32) ** levels(key_list[21], (ADAPTER_TOTAL, ADAPTER_RANK, QUERY_HEADS * HEAD_WIDTH), ((2, 4),), -0.2, 0.2)), 1.346363732307454e-11, 5.385454929229816e-11)
    key_value_first_moment = scatter_about(key_list[22], (ADAPTER_TOTAL, 2, ADAPTER_RANK, KEY_VALUE_HEADS * HEAD_WIDTH), (0.11 / NPARAM ** 0.5), 0.0004272461, (), jnp.float32)
    key_value_second_moment = jnp.clip(jnp.exp(jax.random.uniform(key_list[23], (ADAPTER_TOTAL, 2, ADAPTER_RANK, KEY_VALUE_HEADS * HEAD_WIDTH), jnp.float32, math.log(4.487879234904568e-10), math.log(1.7951516939618273e-09))), 4.487879234904568e-10, 1.7951516939618273e-09)
    output_down_first_moment = scatter_about(key_list[24], (ADAPTER_TOTAL, QUERY_HEADS * HEAD_WIDTH, ADAPTER_RANK), (0.011 / NPARAM ** 0.5), 4.57763671875e-05, ((1, 4),), jnp.float32)
    output_down_second_moment = jnp.clip(jnp.exp(math.log(1.7951517009007212e-11) - 1.3862944 * jax.random.uniform(key_list[25], (ADAPTER_TOTAL, QUERY_HEADS * HEAD_WIDTH, ADAPTER_RANK), jnp.float32) ** levels(key_list[25], (ADAPTER_TOTAL, QUERY_HEADS * HEAD_WIDTH, ADAPTER_RANK), ((1, 4),), -0.2, 0.2)), 4.487879252251803e-12, 1.7951517009007212e-11)
    output_up_first_moment = scatter_about(key_list[26], (ADAPTER_TOTAL, MODEL_WIDTH, ADAPTER_RANK), (0.022 / NPARAM ** 0.5), 9.1552734375e-05, ((1, 8),), jnp.float32)
    output_up_second_moment = jnp.clip(jnp.exp(math.log(7.180606803602885e-11) - 1.3862944 * jax.random.uniform(key_list[27], (ADAPTER_TOTAL, MODEL_WIDTH, ADAPTER_RANK), jnp.float32) ** levels(key_list[27], (ADAPTER_TOTAL, MODEL_WIDTH, ADAPTER_RANK), ((1, 8),), -0.2, 0.2)), 1.7951517009007212e-11, 7.180606803602885e-11)
    routes_keys = jax.random.split(jax.random.fold_in(key_list[28], 1), TOKENS // TOK_DEV)
    routes_turns = jax.random.permutation(jax.random.fold_in(key_list[28], 3), TOKENS // TOK_DEV)
    routes = jax.vmap(lambda own, number: assign_block(jax.random.fold_in(key_list[28], 2), own, number, TOK_DEV, EXPERTS, TOP, CAP, 1))(routes_keys, routes_turns).reshape((TOKENS, TOP))
    tree_adapter_index = with_ends(jax.random.randint(key_list[29], (TREES,), 0, ADAPTER_TOTAL), jax.random.fold_in(key_list[29], 1), 0, ADAPTER_TOTAL - 1).astype(jnp.int32)
    tree_node_length = jax.vmap(lambda own: ragged_sizes(own, NODES, TOK_DEV, TOK_DEV // 2, 1))(jax.random.split(key_list[30], TREES)).reshape((TREES, NODES)).astype(jnp.int32)
    parents = draw_parents(jax.random.fold_in(key_list[32], 71), 0)
    return dict(inputs=inputs, cotangent=cotangent, attention_norm_gain=attention_norm_gain, expert_norm_gain=expert_norm_gain, query_norm_gain=query_norm_gain, key_norm_gain=key_norm_gain, frozen_query_weight=frozen_query_weight, frozen_key_weight=frozen_key_weight, frozen_value_weight=frozen_value_weight, frozen_output_weight=frozen_output_weight, frozen_router_weight=frozen_router_weight, expert_gate_up_weight=expert_gate_up_weight, expert_down_weight=expert_down_weight, adapter_input_down=adapter_input_down, adapter_query_up=adapter_query_up, adapter_key_value_up=adapter_key_value_up, adapter_output_down=adapter_output_down, adapter_output_up=adapter_output_up, input_first_moment=input_first_moment, input_second_moment=input_second_moment, query_first_moment=query_first_moment, query_second_moment=query_second_moment, key_value_first_moment=key_value_first_moment, key_value_second_moment=key_value_second_moment, output_down_first_moment=output_down_first_moment, output_down_second_moment=output_down_second_moment, output_up_first_moment=output_up_first_moment, output_up_second_moment=output_up_second_moment, routes=routes, tree_adapter_index=tree_adapter_index, tree_node_length=tree_node_length, parents=parents)


highest = lax.Precision.HIGHEST
norm_eps = 1e-06
rope_base = 1000000.0
beta_first = 0.9
beta_second = 0.999
adam_eps = 1e-08
decay_rate = 0.01
learning_rate_lower = 0.02
learning_rate_upper = 0.1
learning_rate_output = 0.25
clip_limit = 1.0
masked_score = -1e+30

@jax.custom_vjp
def low(v):
    return lax.optimization_barrier(v.astype(jnp.bfloat16)).astype(jnp.float32)

@jax.custom_vjp
def low_back(v):
    return v

def low_keep(v):
    return (low(v), None)

def low_pass(kept, grad):
    return (grad,)

def back_keep(v):
    return (v, None)

def back_low(kept, grad):
    return (low(grad),)
low.defvjp(low_keep, low_pass)
low_back.defvjp(back_keep, back_low)

def matrix_multiply(left, right):
    return jnp.dot(left, right, precision=highest, preferred_element_type=jnp.float32)

def rms_norm(values, gain):
    return values * lax.rsqrt(lax.optimization_barrier(jnp.mean(values * values, axis=-1, keepdims=True)) + norm_eps) * gain

def rotate(values, positions):
    half_dim = values.shape[-1] // 2
    frequency = rope_base ** (-jnp.arange(half_dim, dtype=jnp.float32) / half_dim)
    angles = positions.astype(jnp.float32)[:, None] * frequency[None, :]
    cosine = jnp.cos(angles)[:, None, :]
    sine_part = jnp.sin(angles)[:, None, :]
    lower_half = values[..., :half_dim]
    upper_half = values[..., half_dim:]
    return jnp.concatenate([lower_half * cosine - upper_half * sine_part, upper_half * cosine + lower_half * sine_part], axis=-1)

def tree_layout(lengths, parents, token_count):
    node_ids = jnp.arange(lengths.shape[0], dtype=jnp.int32)
    node_ends = jnp.cumsum(lengths, dtype=jnp.int32)
    node_starts = node_ends - lengths
    token_ids = jnp.arange(token_count, dtype=jnp.int32)
    node_of = lax.optimization_barrier(jnp.sum((token_ids[:, None] >= node_ends[None, :]).astype(jnp.int32), axis=1, dtype=jnp.int32))
    grandparent = parents[parents]
    ancestor = (node_ids[None, :] == node_ids[:, None]) | (node_ids[None, :] == parents[:, None]) | (node_ids[None, :] == grandparent[:, None])
    strict = ancestor & (node_ids[None, :] != node_ids[:, None])
    before = lax.optimization_barrier(jnp.sum(jnp.where(strict, lengths[None, :], 0), axis=1, dtype=jnp.int32))
    node_hot = node_of[:, None] == node_ids[None, :]
    positions = lax.optimization_barrier(jnp.sum(jnp.where(node_hot, (before - node_starts)[None, :], 0), axis=1, dtype=jnp.int32)) + token_ids
    reachable = ancestor[node_of][:, node_of]
    allowed = reachable & (token_ids[None, :] <= token_ids[:, None])
    return (positions, allowed)

def tree_block(trained_params, frozen, tree):
    adapter_input_down, adapter_query_up, adapter_key_value_up, adapter_output_down, adapter_output_up = trained_params
    attention_norm_gain, expert_norm_gain, query_norm_gain, key_norm_gain, frozen_query_weight, frozen_key_weight, frozen_value_weight, frozen_output_weight, frozen_router_weight, expert_gate_up_weight, expert_down_weight = frozen
    hidden_input, adapter_slot, lengths, parents, routes = tree
    length = hidden_input.shape[0]
    positions, allowed = tree_layout(lengths, parents, length)
    normalized_input = low(rms_norm(hidden_input, attention_norm_gain))
    adapter_middle = low(matrix_multiply(normalized_input, low(adapter_input_down[adapter_slot])))
    key_value_raise = low(adapter_key_value_up[adapter_slot])
    query_projected = low_back(matrix_multiply(normalized_input, frozen_query_weight) + matrix_multiply(adapter_middle[:, :ADAPTER_RANK], low(adapter_query_up[adapter_slot])))
    key_projected = low_back(matrix_multiply(normalized_input, frozen_key_weight) + matrix_multiply(adapter_middle[:, ADAPTER_RANK:2 * ADAPTER_RANK], key_value_raise[0]))
    value_projected = low_back(matrix_multiply(normalized_input, frozen_value_weight) + matrix_multiply(adapter_middle[:, 2 * ADAPTER_RANK:], key_value_raise[1]))
    queries = low(rotate(rms_norm(query_projected.reshape(length, QUERY_HEADS, HEAD_WIDTH), query_norm_gain), positions))
    keys_rot = low(rotate(rms_norm(key_projected.reshape(length, KEY_VALUE_HEADS, HEAD_WIDTH), key_norm_gain), positions))
    values_low = low(value_projected.reshape(length, KEY_VALUE_HEADS, HEAD_WIDTH))
    grouped = queries.reshape(length, KEY_VALUE_HEADS, QUERY_HEADS // KEY_VALUE_HEADS, HEAD_WIDTH)
    raw_scores = jnp.einsum('ikgd,jkd->kgij', grouped, keys_rot, precision=highest) * HEAD_WIDTH ** (-0.5)
    scores = low_back(jnp.where(allowed[None, None], raw_scores, masked_score))
    probs = low(jax.nn.softmax(scores, axis=-1))
    head_rows = low(low_back(jnp.einsum('kgij,jkd->ikgd', probs, values_low, precision=highest))).reshape(length, QUERY_HEADS * HEAD_WIDTH)
    middle_output = low(matrix_multiply(head_rows, low(adapter_output_down[adapter_slot])))
    tree_branch = low_back(matrix_multiply(head_rows, frozen_output_weight) + matrix_multiply(middle_output, low(adapter_output_up[adapter_slot]).T))
    resid = hidden_input + tree_branch
    normed_post = low(rms_norm(resid, expert_norm_gain))
    logits = low_back(matrix_multiply(normed_post, frozen_router_weight))
    chosen = jnp.take_along_axis(logits, routes, axis=1)
    gate_probs = jax.nn.softmax(chosen, axis=-1)
    expert_ids = jnp.arange(EXPERTS, dtype=jnp.int32)
    token_weights = lax.optimization_barrier(jnp.sum(jnp.where(routes[:, :, None] == expert_ids[None, None, :], gate_probs[:, :, None], 0.0), axis=1))

    def expert(operands):
        gate_up, down_proj, column = operands
        projected = low_back(matrix_multiply(normed_post, gate_up))
        inner_act = low(jax.nn.silu(projected[:, :F]) * projected[:, F:])
        return low_back(matrix_multiply(inner_act, down_proj)) * column[:, None]
    expert_out = lax.map(jax.checkpoint(expert), (expert_gate_up_weight, expert_down_weight, token_weights.T))
    mixture = lax.optimization_barrier(jnp.sum(expert_out, axis=0))
    return (resid + mixture, mixture)

def moment_update(weight, first, second, grad, rate):
    first = beta_first * first + (1.0 - beta_first) * grad
    second = beta_second * second + (1.0 - beta_second) * grad * grad
    first_hat = first / (1.0 - beta_first ** STEP)
    second_hat = second / (1.0 - beta_second ** STEP)
    weight = weight - rate * (first_hat / (jnp.sqrt(second_hat) + adam_eps) + decay_rate * weight)
    return (weight, first, second)

def reference(inputs, cotangent, attention_norm_gain, expert_norm_gain, query_norm_gain, key_norm_gain, frozen_query_weight, frozen_key_weight, frozen_value_weight, frozen_output_weight, frozen_router_weight, expert_gate_up_weight, expert_down_weight, adapter_input_down, adapter_query_up, adapter_key_value_up, adapter_output_down, adapter_output_up, input_first_moment, input_second_moment, query_first_moment, query_second_moment, key_value_first_moment, key_value_second_moment, output_down_first_moment, output_down_second_moment, output_up_first_moment, output_up_second_moment, routes, tree_adapter_index, tree_node_length, parents):
    frozen = (attention_norm_gain.astype(jnp.float32), expert_norm_gain.astype(jnp.float32), query_norm_gain.astype(jnp.float32), key_norm_gain.astype(jnp.float32), frozen_query_weight.astype(jnp.float32), frozen_key_weight.astype(jnp.float32), frozen_value_weight.astype(jnp.float32), frozen_output_weight.astype(jnp.float32), frozen_router_weight.astype(jnp.float32), expert_gate_up_weight.astype(jnp.float32), expert_down_weight.astype(jnp.float32))
    tree_data = (tree_adapter_index, tree_node_length, parents, routes.reshape(TREES, TOK_DEV, TOP))

    def forward_pass(adapter_input_down, adapter_query_up, adapter_key_value_up, adapter_output_down, adapter_output_up, hidden_input):
        trained_params = (adapter_input_down, adapter_query_up, adapter_key_value_up, adapter_output_down, adapter_output_up)

        def visit(carry, tree):
            return (carry, jax.checkpoint(tree_block)(trained_params, frozen, tree))
        blocks = (hidden_input.reshape(TREES, TOK_DEV, MODEL_WIDTH),) + tree_data
        carry, outputs = lax.scan(visit, jnp.zeros((), jnp.float32), blocks)
        return (outputs[0].reshape(TOKENS, MODEL_WIDTH), outputs[1].reshape(TOKENS, MODEL_WIDTH))
    layer_output, backward_map, expert_output = jax.vjp(forward_pass, adapter_input_down, adapter_query_up, adapter_key_value_up, adapter_output_down, adapter_output_up, inputs.astype(jnp.float32), has_aux=True)
    gradient_tree = backward_map(cotangent.astype(jnp.float32))
    input_grad = gradient_tree[5]
    total = jnp.sum(gradient_tree[0] * gradient_tree[0]) + jnp.sum(gradient_tree[1] * gradient_tree[1]) + jnp.sum(gradient_tree[2] * gradient_tree[2]) + jnp.sum(gradient_tree[3] * gradient_tree[3]) + jnp.sum(gradient_tree[4] * gradient_tree[4])
    grad_norm = jnp.sqrt(total)
    scale_factor = jnp.minimum(1.0, clip_limit / (grad_norm + 1e-06))
    input_following = moment_update(adapter_input_down, input_first_moment, input_second_moment, gradient_tree[0] * scale_factor, learning_rate_lower)
    query_following = moment_update(adapter_query_up, query_first_moment, query_second_moment, gradient_tree[1] * scale_factor, learning_rate_upper)
    key_value_following = moment_update(adapter_key_value_up, key_value_first_moment, key_value_second_moment, gradient_tree[2] * scale_factor, learning_rate_upper)
    down_following = moment_update(adapter_output_down, output_down_first_moment, output_down_second_moment, gradient_tree[3] * scale_factor, learning_rate_output)
    up_following = moment_update(adapter_output_up, output_up_first_moment, output_up_second_moment, gradient_tree[4] * scale_factor, learning_rate_upper)
    return (layer_output, input_grad, grad_norm, input_following[0], input_following[1], input_following[2], query_following[0], query_following[1], query_following[2], key_value_following[0], key_value_following[1], key_value_following[2], down_following[0], down_following[1], down_following[2], up_following[0], up_following[1], up_following[2], expert_output)
```

```python
import functools

import jax
import jax.numpy as jnp
from jax import lax
from jax.experimental import pallas as pl
from jax.experimental.pallas import tpu as pltpu
from jax.sharding import PartitionSpec as P

HEAD_WIDTH = 128
STEP = 10


norm_eps = 1e-06
rope_base = 1000000.0
beta_first = 0.9
beta_second = 0.999
adam_eps = 1e-08
decay_rate = 0.01
learning_rate_lower = 0.02
learning_rate_upper = 0.1
learning_rate_output = 0.25
clip_limit = 1.0
masked_score = -1e30
score_scale = HEAD_WIDTH ** (-0.5)
low = jnp.bfloat16
wide = jnp.float32


def contract_last(left, right):
    return lax.dot_general(left, right, (((1,), (1,)), ((), ())), preferred_element_type=wide)


def contract_leading(left, right):
    return lax.dot_general(left, right, (((0,), (0,)), ((), ())), preferred_element_type=wide)


def product(left, right):
    return jnp.dot(left, right, preferred_element_type=wide)


def rms_norm(values, gain):
    return values * lax.rsqrt(jnp.mean(values * values, axis=-1, keepdims=True) + norm_eps) * gain


def moment_update(weight, first, second, grad, rate):
    first = beta_first * first + (1.0 - beta_first) * grad
    second = beta_second * second + (1.0 - beta_second) * grad * grad
    first_hat = first / (1.0 - beta_first**STEP)
    second_hat = second / (1.0 - beta_second**STEP)
    weight = weight - rate * (first_hat / (jnp.sqrt(second_hat) + adam_eps) + decay_rate * weight)
    return (weight, first, second)


def nought(values):
    return jnp.isnan(values[0, 0].astype(wide)).astype(jnp.int32)


def held(kernel, inputs, waits):
    def run(*refs):
        return kernel(*refs[:inputs], *refs[inputs + waits :])

    return run


anywhere = pl.BlockSpec(memory_space=pl.ANY)


def project_kernel(turned, left_ref, weight_ref, thin_ref, thin_weight_ref, out_ref):
    whole = contract_last if turned else product
    total = whole(left_ref[...], weight_ref[...]) + product(thin_ref[...], thin_weight_ref[...])
    out_ref[...] = total.astype(out_ref.dtype)


def project(left, weight, thin, thin_weight, turned, dtype, waits=()):
    tokens, depth = left.shape
    cols = weight.shape[0 if turned else 1]
    rank = thin.shape[1]
    block = 512 if depth <= 2048 else 256
    if turned:
        weight_spec = pl.BlockSpec((block, depth), lambda j: (j, 0))
    else:
        weight_spec = pl.BlockSpec((depth, block), lambda j: (0, j))
    return pl.pallas_call(
        held(functools.partial(project_kernel, turned), 4, len(waits)),
        grid=(cols // block,),
        in_specs=[
            pl.BlockSpec((tokens, depth), lambda j: (0, 0)),
            weight_spec,
            pl.BlockSpec((tokens, rank), lambda j: (0, 0)),
            pl.BlockSpec((rank, block), lambda j: (0, j)),
            *[anywhere] * len(waits),
        ],
        out_specs=pl.BlockSpec((tokens, block), lambda j: (0, j)),
        out_shape=jax.ShapeDtypeStruct((tokens, cols), dtype),
        compiler_params=pltpu.CompilerParams(vmem_limit_bytes=60 << 20),
        cost_estimate=pl.CostEstimate(flops=0, bytes_accessed=0, transcendentals=0),
        name="project",
    )(left, weight, thin, thin_weight, *waits)


def shift(values, step):
    count = lax.axis_size("col")
    pairs = [(i, (i + step) % count) for i in range(count)]
    return lax.ppermute(values, "col", pairs)


def ring_gather(values):
    parts = [values]
    for _ in range(lax.axis_size("col") - 1):
        parts.append(shift(parts[-1], 1))
    return parts


def origin(k):
    count = lax.axis_size("col")
    return lax.rem(lax.axis_index("col") + count - k, count)


def in_order(parts, axis, wait=0):
    size = parts[0].shape[axis]
    shape = list(parts[0].shape)
    shape[axis] = size * len(parts)
    out = jnp.zeros(shape, parts[0].dtype)
    for k, part in enumerate(parts):
        out = lax.dynamic_update_slice_in_dim(out, part, origin(k) * size + wait, axis)
    return out


def ring_scatter(part_of):
    count = lax.axis_size("col")
    total = part_of(origin(1))
    for k in range(1, count):
        total = shift(total.astype(low), 1).astype(wide) + part_of(origin(k + 1))
    return total


def exchange(piece_of):
    count = lax.axis_size("col")
    return [piece_of(origin(0))] + [shift(piece_of(origin(count - k)), k) for k in range(1, count)]


def tree_sum(parts):
    if len(parts) == 1:
        return parts[0].astype(wide)
    return tree_sum(parts[0::2]) + tree_sum(parts[1::2])


def hop_kernel(arrives, count, *refs):
    arrived, own, out_ref = refs[1 : 1 + arrives], refs[1 + arrives : 1 + arrives + count], refs[-1]
    start = 0
    for ref in own:
        span = pl.ds(start, ref.shape[1])
        total = ref[...].astype(wide)
        if arrives:
            total = total + arrived[0][:, span].astype(wide)
        out_ref[:, span] = total.astype(out_ref.dtype)
        start += ref.shape[1]


def hop(place, arrived, own, block, dtype, waits=()):
    rows, cols = block
    across = own[0].shape[1] != cols
    step = min(rows, 256 if across else 64)
    steps = rows // step
    total = cols * len(own)

    def whole(i, p):
        return (i, 0)

    def mine(i, p):
        return (i, p[0]) if across else (p[0] * steps + i, 0)

    arrivals = () if arrived is None else (arrived,)
    return pl.pallas_call(
        held(functools.partial(hop_kernel, len(arrivals), len(own)), 1 + len(arrivals) + len(own), len(waits)),
        grid_spec=pltpu.PrefetchScalarGridSpec(
            num_scalar_prefetch=1,
            grid=(steps,),
            in_specs=[pl.BlockSpec((step, total), whole)] * len(arrivals)
            + [pl.BlockSpec((step, cols), mine)] * len(own)
            + [anywhere] * len(waits),
            out_specs=pl.BlockSpec((step, total), whole),
        ),
        out_shape=jax.ShapeDtypeStruct((rows, total), dtype),
        compiler_params=pltpu.CompilerParams(vmem_limit_bytes=60 << 20),
        name="hop",
    )(place.reshape(1), *arrivals, *own, *waits)


def sum_kernel(*refs):
    refs[-1][...] = tree_sum([ref[...] for ref in refs[:-1]]).astype(refs[-1].dtype)


def summed(parts, waits):
    shape = parts[0].shape
    return pl.pallas_call(
        held(sum_kernel, len(parts), len(waits)),
        grid=(1,),
        in_specs=[pl.BlockSpec(shape, lambda i: (0, 0))] * len(parts) + [anywhere] * len(waits),
        out_specs=pl.BlockSpec(shape, lambda i: (0, 0)),
        out_shape=jax.ShapeDtypeStruct(shape, parts[0].dtype),
        compiler_params=pltpu.CompilerParams(vmem_limit_bytes=60 << 20),
        name="summed",
    )(*parts, *waits)


def head_forward(proj, gain, cos, sin):
    inv = lax.rsqrt(jnp.mean(proj * proj, axis=-1, keepdims=True) + norm_eps)
    scaled = proj * inv * gain
    return scaled * cos + pltpu.roll(scaled, HEAD_WIDTH // 2, 1) * sin, inv


def attend_kernel(share, proj_ref, cos_ref, sin_ref, gain_ref, bias_ref, key_ref, value_ref,
                  out_ref, lse_ref, value_t):
    @pl.when(lax.rem(pl.program_id(0), share) == 0)
    def _():
        value_t[...] = value_ref[...].T

    query, _ = head_forward(proj_ref[...], gain_ref[...], cos_ref[...], sin_ref[...])
    scores = contract_last(key_ref[...], query.astype(low)) * score_scale + bias_ref[...]
    top = jnp.max(scores, axis=0, keepdims=True)
    probs = jnp.exp(scores - top)
    total = jnp.sum(probs, axis=0, keepdims=True)
    mixed = product(value_t[...], probs.astype(low)) / total
    out_ref[...] = mixed.T.astype(low)
    lse_ref[0] = top + jnp.log(total)


def attend_back_kernel(share, proj_ref, cos_ref, sin_ref, gain_ref, bias_ref, key_ref, value_ref,
                       lse_ref, branch_ref, weight_ref, middle_ref, down_ref,
                       out_ref, key_grad_ref, value_grad_ref, key_t):
    @pl.when(lax.rem(pl.program_id(0), share) == 0)
    def _():
        key_t[...] = key_ref[...].T
        key_grad_ref[...] = jnp.zeros_like(key_grad_ref)
        value_grad_ref[...] = jnp.zeros_like(value_grad_ref)

    proj, gain, cos, sin = proj_ref[...], gain_ref[...], cos_ref[...], sin_ref[...]
    query, inv = head_forward(proj, gain, cos, sin)
    query = query.astype(low)
    grad = contract_last(branch_ref[...], weight_ref[...])
    grad = (grad + product(middle_ref[...], down_ref[...])).astype(low)
    scores = contract_last(key_ref[...], query) * score_scale + bias_ref[...]
    probs = jnp.exp(scores - lse_ref[0])
    probs_grad = contract_last(value_ref[...], grad)
    delta = jnp.sum(probs * probs_grad, axis=0, keepdims=True)
    scores_grad = (probs * (probs_grad - delta)).astype(low)
    value_grad_ref[...] += product(probs.astype(low), grad)
    key_grad_ref[...] += product(scores_grad, query) * score_scale
    rotated = product(key_t[...], scores_grad).T * score_scale
    scaled = rotated * cos + pltpu.roll(rotated * sin, HEAD_WIDTH // 2, 1)
    scaled = scaled * gain
    slope = jnp.mean(scaled * proj, axis=-1, keepdims=True)
    out_ref[...] = (inv * scaled - proj * (inv * inv * inv * slope)).astype(low)


def head_specs(tokens, length, first, share, kv_total):
    def head(h):
        return (0, first + h)

    def fixed(h):
        return (0, 0)

    return [
        pl.BlockSpec((tokens, HEAD_WIDTH), head),
        pl.BlockSpec((tokens, HEAD_WIDTH), fixed),
        pl.BlockSpec((tokens, HEAD_WIDTH), fixed),
        pl.BlockSpec((1, HEAD_WIDTH), fixed),
        pl.BlockSpec((length, tokens), fixed),
        pl.BlockSpec((length, HEAD_WIDTH), lambda h: (0, (first + h) // share)),
        pl.BlockSpec((length, HEAD_WIDTH), lambda h: (0, kv_total + (first + h) // share)),
    ]


def attend_cost(products, tokens, length, heads):
    return pl.CostEstimate(
        flops=4 * products * tokens * length * heads * HEAD_WIDTH,
        bytes_accessed=8 * tokens * heads * HEAD_WIDTH,
        transcendentals=tokens * length * heads,
    )


def attend(proj, cos, sin, gain, bias, keys_values):
    tokens, cols = proj.shape
    length, heads = keys_values.shape[0], cols // HEAD_WIDTH
    kv_total = keys_values.shape[1] // (2 * HEAD_WIDTH)
    share = heads // kv_total
    return pl.pallas_call(
        functools.partial(attend_kernel, share),
        grid=(heads,),
        in_specs=head_specs(tokens, length, 0, share, kv_total),
        out_specs=[
            pl.BlockSpec((tokens, HEAD_WIDTH), lambda h: (0, h)),
            pl.BlockSpec((1, 1, tokens), lambda h: (h, 0, 0)),
        ],
        scratch_shapes=[pltpu.VMEM((HEAD_WIDTH, length), low)],
        out_shape=[
            jax.ShapeDtypeStruct((tokens, cols), low),
            jax.ShapeDtypeStruct((heads, 1, tokens), wide),
        ],
        compiler_params=pltpu.CompilerParams(vmem_limit_bytes=60 << 20),
        cost_estimate=attend_cost(3, tokens, length, heads),
        name="attend",
    )(proj, cos, sin, gain, bias, keys_values, keys_values)


def attend_back(part, parts, proj, cos, sin, gain, bias, keys_values, lse, branch, weight, middle, down,
                filled, waits):
    tokens, length = proj.shape[0], keys_values.shape[0]
    total, width, rank = proj.shape[1] // HEAD_WIDTH, branch.shape[1], middle.shape[1]
    kv_total = keys_values.shape[1] // (2 * HEAD_WIDTH)
    share, heads = total // kv_total, total // parts
    first = part * heads

    def fixed(h):
        return (0, 0)

    def head(h):
        return (0, first + h)

    def kv_head(h):
        return (0, (first + h) // share)

    return pl.pallas_call(
        held(functools.partial(attend_back_kernel, share), 12, len(filled) + len(waits)),
        grid=(heads,),
        in_specs=head_specs(tokens, length, first, share, kv_total)
        + [
            pl.BlockSpec((1, 1, tokens), lambda h: (first + h, 0, 0)),
            pl.BlockSpec((tokens, width), fixed),
            pl.BlockSpec((HEAD_WIDTH, width), lambda h: (first + h, 0)),
            pl.BlockSpec((tokens, rank), fixed),
            pl.BlockSpec((rank, HEAD_WIDTH), head),
            *[anywhere] * (len(filled) + len(waits)),
        ],
        out_specs=[
            pl.BlockSpec((tokens, HEAD_WIDTH), head),
            pl.BlockSpec((length, HEAD_WIDTH), kv_head),
            pl.BlockSpec((length, HEAD_WIDTH), kv_head),
        ],
        scratch_shapes=[pltpu.VMEM((HEAD_WIDTH, length), low)],
        out_shape=[
            jax.ShapeDtypeStruct(proj.shape, low),
            jax.ShapeDtypeStruct((length, kv_total * HEAD_WIDTH), wide),
            jax.ShapeDtypeStruct((length, kv_total * HEAD_WIDTH), wide),
        ],
        input_output_aliases={12 + i: i for i in range(len(filled))},
        compiler_params=pltpu.CompilerParams(vmem_limit_bytes=60 << 20),
        cost_estimate=pl.CostEstimate(flops=0, bytes_accessed=0, transcendentals=0),
        name="attend_back",
    )(proj, cos, sin, gain, bias, keys_values, keys_values, lse, branch, weight, middle, down, *filled, *waits)


def experts_kernel(place_ref, normed_ref, back_ref, weight_ref, gate_ref, up_ref, down_ref,
                   post_ref, out_ref, out_sum):
    e = pl.program_id(0)
    width = normed_ref.shape[1]

    @pl.when(e == 0)
    def _():
        post_ref[...] = jnp.zeros_like(post_ref)
        out_sum[...] = jnp.zeros_like(out_sum)

    normed = normed_ref[...]
    gate = product(normed, gate_ref[0])
    up = product(normed, up_ref[0])
    back = back_ref[...]
    weights = weight_ref[...]
    lane = lax.broadcasted_iota(jnp.int32, weights.shape, 1)
    weight = jnp.sum(jnp.where(lane == e, weights, 0.0), axis=1, keepdims=True)
    sig = jax.nn.sigmoid(gate)
    act = gate * sig
    inner = act * up
    lane = lax.broadcasted_iota(jnp.int32, (normed.shape[0], HEAD_WIDTH), 1)
    gate_sum = jnp.sum(inner * back, axis=1, keepdims=True)
    post_ref[:, width:] += jnp.where(lane == place_ref[1] + e, gate_sum, 0.0)
    back = back * weight
    gate_grad = (back * up * (sig + act * (1.0 - sig))).astype(low)
    up_grad = (back * act).astype(low)
    out_sum[...] += product((inner * weight).astype(low), down_ref[...])
    post_ref[:, :width] += contract_last(gate_grad, gate_ref[0]) + contract_last(up_grad, up_ref[0])

    @pl.when(e == pl.num_programs(0) - 1)
    def _():
        out_ref[...] = out_sum[...].astype(low)


def experts(chunk, first_expert, tokens, normed, back, weights, gate_up, down, mixture, waits):
    filled = () if mixture is None else (mixture,)
    waits = (*filled, *waits)
    width = normed.shape[1]
    count, inner_width = gate_up.shape[0], gate_up.shape[2] // 2
    return pl.pallas_call(
        held(experts_kernel, 7, len(waits)),
        grid_spec=pltpu.PrefetchScalarGridSpec(
            num_scalar_prefetch=1,
            grid=(count,),
            in_specs=[
                pl.BlockSpec((tokens, width), lambda e, p: (p[0], 0)),
                pl.BlockSpec((tokens, inner_width), lambda e, p: (p[0], e)),
                pl.BlockSpec((tokens, count), lambda e, p: (p[0], 0)),
                pl.BlockSpec((1, width, inner_width), lambda e, p: (e, 0, 0)),
                pl.BlockSpec((1, width, inner_width), lambda e, p: (e, 0, 1)),
                pl.BlockSpec((inner_width, width), lambda e, p: (e, 0)),
                *[anywhere] * len(waits),
            ],
            out_specs=[
                pl.BlockSpec((tokens, width + HEAD_WIDTH), lambda e, p: (0, 0)),
                pl.BlockSpec((tokens, width), lambda e, p: (p[0], 0)),
            ],
            scratch_shapes=[pltpu.VMEM((tokens, width), wide)],
        ),
        out_shape=[
            jax.ShapeDtypeStruct((tokens, width + HEAD_WIDTH), wide),
            jax.ShapeDtypeStruct(normed.shape, low),
        ],
        input_output_aliases={7: 1} if filled else {},
        compiler_params=pltpu.CompilerParams(vmem_limit_bytes=60 << 20),
        cost_estimate=pl.CostEstimate(
            flops=10 * tokens * width * count * inner_width,
            bytes_accessed=6 * width * count * inner_width,
            transcendentals=tokens * count * inner_width,
        ),
        name="experts",
    )(jnp.stack([chunk, first_expert]), normed, back, weights, gate_up, gate_up, down, *waits)


def settle_kernel(arrived_ref, post_ref, probs_ref, router_ref, resid_ref, gain_ref, cot_ref, up_ref,
                  grad_ref, branch_ref, middle_ref):
    width = resid_ref.shape[1]
    gate_grad = arrived_ref[:, width:].astype(wide) + post_ref[:, width:]
    probs = probs_ref[...]
    logits_grad = probs * (gate_grad - jnp.sum(probs * gate_grad, axis=1, keepdims=True))
    grad = arrived_ref[:, :width].astype(wide) + post_ref[:, :width]
    grad = (grad + product(logits_grad.astype(low), router_ref[...])) * gain_ref[...]
    resid = resid_ref[...]
    inv = lax.rsqrt(jnp.mean(resid * resid, axis=1, keepdims=True) + norm_eps)
    slope = jnp.mean(grad * resid, axis=1, keepdims=True)
    grad = cot_ref[...].astype(wide) + inv * grad - resid * (inv * inv * inv * slope)
    grad_ref[...] = grad
    branch = grad.astype(low)
    branch_ref[...] = branch
    middle_ref[...] = contract_last(branch, up_ref[...]).astype(low)


def settle(arrived, post, probs, router, resid, gain, cot, up):
    tokens, width = resid.shape
    rank = up.shape[0]
    block = min(tokens, 64)
    lanes = arrived.shape[1] - width

    def rows(cols):
        return pl.BlockSpec((block, cols), lambda i: (i, 0))

    def whole(*shape):
        return pl.BlockSpec(shape, lambda i: (0, 0))

    return pl.pallas_call(
        settle_kernel,
        grid=(tokens // block,),
        in_specs=[
            rows(width + lanes),
            rows(width + lanes),
            rows(lanes),
            whole(lanes, width),
            rows(width),
            whole(1, width),
            rows(width),
            whole(rank, width),
        ],
        out_specs=[rows(width), rows(width), rows(rank)],
        out_shape=[
            jax.ShapeDtypeStruct((tokens, width), wide),
            jax.ShapeDtypeStruct((tokens, width), low),
            jax.ShapeDtypeStruct((tokens, rank), low),
        ],
        compiler_params=pltpu.CompilerParams(vmem_limit_bytes=60 << 20),
        cost_estimate=pl.CostEstimate(flops=0, bytes_accessed=0, transcendentals=0),
        name="settle",
    )(arrived, post, probs, router, resid, gain, cot, up)


def update_kernel(rates, count, slot_ref, square_ref, *refs):
    size = len(rates)
    whole, own = refs[:count], refs[count : count + size]
    state = refs[count + size : count + 4 * size]
    norm_ref = refs[count + 4 * size]
    outs = refs[count + 4 * size + 1 : count + 7 * size + 1]
    sums, factor_ref = refs[count + 7 * size + 1 : -1], refs[-1]
    now = pl.program_id(0)

    @pl.when(now == 0)
    def _():
        total = square_ref[...]
        for trees_ref, sum_ref in zip((*whole, *own), sums):
            sum_ref[...] = jnp.zeros_like(sum_ref)

            def tree(t, carry, trees_ref=trees_ref, sum_ref=sum_ref):
                at = slot_ref[t]
                sum_ref[at] += trees_ref[t].astype(wide)
                return carry

            lax.fori_loop(0, trees_ref.shape[0], tree, 0)
        for sum_ref in sums[:count]:

            def square(s, carry, sum_ref=sum_ref):
                part = jnp.sum(sum_ref[s] * sum_ref[s], axis=0, keepdims=True)
                return carry + jnp.sum(part, axis=1, keepdims=True)

            total = lax.fori_loop(0, sum_ref.shape[0], square, total)
        norm = jnp.sqrt(total)
        norm_ref[...] = norm
        factor_ref[...] = jnp.minimum(1.0, clip_limit / (norm + 1e-06))

    factor = factor_ref[...]
    for i, rate in enumerate(rates):
        weight, first, second = (ref[0] for ref in state[3 * i : 3 * i + 3])
        new = moment_update(weight, first, second, sums[count + i][now] * factor, rate)
        for ref, value in zip(outs[3 * i : 3 * i + 3], new):
            ref[0] = value


def update(slots, square, whole, own, states, rates):
    state = [array for triple in states for array in triple]
    adapters = state[0].shape[0]

    def all_of(array):
        return pl.BlockSpec(array.shape, lambda s: (0,) * array.ndim)

    def one_of(array):
        return pl.BlockSpec((1, *array.shape[1:]), lambda s: (s, 0, 0))

    out = pl.pallas_call(
        functools.partial(update_kernel, tuple(rates), len(whole)),
        grid=(adapters,),
        in_specs=[pl.BlockSpec(memory_space=pltpu.SMEM)]
        + [all_of(a) for a in (square, *whole, *own)]
        + [one_of(a) for a in state],
        out_specs=[all_of(square)] + [one_of(a) for a in state],
        out_shape=[jax.ShapeDtypeStruct((1, 1), wide)]
        + [jax.ShapeDtypeStruct(a.shape, wide) for a in state],
        scratch_shapes=[pltpu.VMEM((adapters, *a.shape[1:]), wide) for a in (*whole, *own)]
        + [pltpu.VMEM((1, 1), wide)],
        compiler_params=pltpu.CompilerParams(vmem_limit_bytes=60 << 20),
        name="update",
    )(slots, square, *whole, *own, *state)
    return out[0], [out[1 + 3 * i : 4 + 3 * i] for i in range(len(states))]


def tree_layout(lengths, parents, token_count, first, count):
    nodes = lengths.shape[0]
    node_ids = jnp.arange(nodes, dtype=jnp.int32)
    node_ends = jnp.cumsum(lengths, dtype=jnp.int32)
    node_starts = node_ends - lengths
    parent_hot = parents[:, None] == node_ids[None, :]
    eye = node_ids[:, None] == node_ids[None, :]
    grand_hot = jnp.any(parent_hot[:, :, None] & parent_hot[None, :, :], axis=1)
    ancestor = eye | parent_hot | grand_hot
    before = jnp.sum(jnp.where(ancestor & ~eye, lengths[None, :], 0), axis=1, dtype=jnp.int32)

    def hot_of(tokens):
        return (tokens[:, None] >= node_starts[None, :]) & (tokens[:, None] < node_ends[None, :])

    keys = jnp.arange(token_count, dtype=jnp.int32)
    queries = first + jnp.arange(count, dtype=jnp.int32)
    query_hot = hot_of(queries)
    positions = queries + jnp.sum(
        jnp.where(query_hot, (before - node_starts)[None, :], 0), axis=1, dtype=jnp.int32
    )
    reach = product(query_hot.astype(low), ancestor.astype(low)).astype(low)
    reachable = contract_last(hot_of(keys).astype(low), reach) > 0.5
    allowed = reachable & (keys[:, None] <= queries[None, :])
    return positions, jnp.where(allowed, 0.0, masked_score)


def shards(
    inputs,
    cotangent,
    attention_norm_gain,
    expert_norm_gain,
    query_norm_gain,
    key_norm_gain,
    frozen_query_weight,
    frozen_key_weight,
    frozen_value_weight,
    frozen_output_weight,
    frozen_router_weight,
    expert_gate_up_weight,
    expert_down_weight,
    adapter_input_down,
    adapter_query_up,
    adapter_key_value_up,
    adapter_output_down,
    adapter_output_up,
    input_first_moment,
    input_second_moment,
    query_first_moment,
    query_second_moment,
    key_value_first_moment,
    key_value_second_moment,
    output_down_first_moment,
    output_down_second_moment,
    output_up_first_moment,
    output_up_second_moment,
    routes,
    tree_adapter_index,
    tree_node_length,
    parents,
):
    col_count = lax.axis_size("col")
    row_count = lax.axis_size("row")
    col_index = lax.axis_index("col")
    row_index = lax.axis_index("row")
    length, col_width = inputs.shape
    width = col_width * col_count
    tokens = length // col_count
    first_token = col_index * tokens
    row_width = frozen_key_weight.shape[0]
    group_cols = frozen_query_weight.shape[1]
    kv_total = frozen_key_weight.shape[1] // HEAD_WIDTH
    kv_cols = kv_total * HEAD_WIDTH
    rank = adapter_query_up.shape[1]
    adapters = adapter_input_down.shape[0]
    local_experts = expert_gate_up_weight.shape[0]
    expert_total = frozen_router_weight.shape[1]
    inner_width = expert_down_weight.shape[1]
    slot = tree_adapter_index[0]

    def gather_rows(values, axis):
        return lax.all_gather(values, "row", axis=axis, tiled=True)

    local_inner = local_experts * inner_width
    first = gather_rows(
        jnp.concatenate(
            [
                expert_down_weight.reshape(local_inner, row_width),
                adapter_input_down.transpose(0, 2, 1).reshape(-1, row_width).astype(low),
                adapter_output_up.transpose(0, 2, 1).reshape(-1, row_width).astype(low),
                frozen_router_weight.T,
                jnp.broadcast_to(slot.astype(low), (16, row_width)),
                frozen_key_weight.T,
                frozen_value_weight.T,
            ]
        ),
        1,
    )
    in_start = local_inner
    up_start = in_start + adapters * 3 * rank
    router_start = up_start + adapters * rank
    slot_start = router_start + expert_total
    kv_start = slot_start + 16
    down_input = lax.dynamic_slice_in_dim(first, in_start + slot * 3 * rank, 3 * rank, 0)
    up_output = lax.dynamic_slice_in_dim(first, up_start + slot * rank, rank, 0)
    router = first[router_start:slot_start]
    slots = first[slot_start, ::row_width].astype(jnp.int32)
    key_value_weight = first[kv_start:]
    query_weight = gather_rows(in_order(ring_gather(frozen_query_weight), 1), 0)
    out_weight = gather_rows(in_order(ring_gather(frozen_output_weight), 0), 1)
    gate_up_weight = gather_rows(expert_gate_up_weight, 1)
    head_adapters = in_order(
        ring_gather(
            jnp.concatenate([adapter_query_up[slot], adapter_output_down[slot].T]).astype(low)
        ),
        1,
    )
    query_raise = head_adapters[:rank]
    down_output = head_adapters[rank:]
    key_value_raise = adapter_key_value_up[slot].astype(low)

    pieces = exchange(lambda c: lax.dynamic_slice_in_dim(inputs, c * tokens, tokens, 0))
    hidden_input = in_order(pieces, 1).astype(wide)
    cot_full = in_order(ring_gather(cotangent), 1)
    cot_own = lax.dynamic_slice_in_dim(cot_full, first_token, tokens, 0)
    positions, bias = tree_layout(tree_node_length[0], parents[0], length, first_token, tokens)

    def norm_in(values):
        return rms_norm(values, attention_norm_gain)

    normalized, norm_in_back = jax.vjp(norm_in, hidden_input)
    normalized = normalized.astype(low)
    middle = contract_last(normalized, down_input).astype(low)
    half = HEAD_WIDTH // 2
    frequency = rope_base ** (-jnp.arange(half, dtype=wide) / half)
    angles = positions.astype(wide)[:, None] * frequency[None, :]
    cos = jnp.concatenate([jnp.cos(angles)] * 2, axis=1)
    sin = jnp.concatenate([-jnp.sin(angles), jnp.sin(angles)], axis=1)

    def shape_keys(proj):
        parts = []
        for head in range(kv_total):
            scaled = rms_norm(proj[:, head * HEAD_WIDTH : (head + 1) * HEAD_WIDTH], key_norm_gain)
            turned = jnp.concatenate([scaled[:, half:], scaled[:, :half]], axis=1)
            parts.append(scaled * cos + turned * sin)
        return jnp.concatenate(parts, axis=1)

    key_value_proj = contract_last(normalized, key_value_weight)
    key_proj = key_value_proj[:, :kv_cols] + product(middle[:, rank : 2 * rank], key_value_raise[0])
    value_proj = key_value_proj[:, kv_cols:] + product(middle[:, 2 * rank :], key_value_raise[1])
    key_rot, keys_back = jax.vjp(shape_keys, key_proj)
    keys_values = in_order(
        ring_gather(jnp.concatenate([key_rot.astype(low), value_proj.astype(low)], axis=1)), 0
    )
    query_gain = query_norm_gain[None, :]
    proj = project(normalized, query_weight, middle[:, :rank], query_raise, False, wide)
    heads, totals = attend(proj, cos, sin, query_gain, bias, keys_values)
    inner_back = contract_last(cot_full, first[:local_inner])
    middle_output = contract_last(heads, down_output).astype(low)
    resid = hidden_input + project(
        heads, out_weight, middle_output, up_output, False, wide, (inner_back,)
    )

    resid_full = in_order(ring_gather(resid.astype(low)), 0)
    normed_post = rms_norm(resid_full.astype(wide), expert_norm_gain).astype(low)
    logits = contract_last(normed_post, router)
    expert_ids = jnp.arange(expert_total, dtype=jnp.int32)
    chosen = jnp.any(routes[:, :, None] == expert_ids[None, None, :], axis=1)
    shifted = logits - jnp.max(jnp.where(chosen, logits, -jnp.inf), axis=1, keepdims=True)
    raised = jnp.where(chosen, jnp.exp(jnp.where(chosen, shifted, 0.0)), 0.0)
    gate_probs = raised / jnp.sum(raised, axis=1, keepdims=True)
    local_probs = lax.dynamic_slice_in_dim(gate_probs, col_index * local_experts, local_experts, 1)
    own_probs = jnp.pad(
        lax.dynamic_slice_in_dim(gate_probs, first_token, tokens, 0),
        ((0, 0), (0, HEAD_WIDTH - expert_total)),
    )
    router_rows = jnp.pad(router, ((0, HEAD_WIDTH - expert_total), (0, 0)))
    local_in = down_input[rank:]
    mixture, arrived, sent = None, None, ()
    for k in range(col_count):
        post, mixture = experts(
            origin(k + 1),
            col_index * local_experts,
            tokens,
            normed_post,
            inner_back,
            local_probs,
            gate_up_weight,
            first,
            mixture,
            sent if k < col_count - 1 else (*sent, own_probs, router_rows, cot_own, local_in),
        )
        if k < col_count - 1:
            sent = ((post if k == 0 else arrived.astype(wide) + post).astype(low),)
            arrived = shift(sent[0], 1)

    def mixture_hop(k, arrived, dtype, *waits):
        return hop(origin(k), arrived, (mixture,), (length, col_width), dtype, waits)

    resid_grad, branch_grad, mid_out_grad = settle(
        arrived, post, own_probs, router_rows, resid, expert_norm_gain[None, :], cot_own, up_output
    )
    mixture_sent = mixture_hop(1, None, low, arrived)
    filled = ()
    for part in range(4):
        waits = ()
        if part in (1, 3):
            mixture_sent = mixture_hop(part // 2 + 2, shift(mixture_sent, 1), low, filled[0])
            waits = (mixture_sent,)
        filled = attend_back(
            part,
            4,
            proj,
            cos,
            sin,
            query_gain,
            bias,
            keys_values,
            totals,
            branch_grad,
            out_weight,
            mid_out_grad,
            down_output,
            filled,
            waits,
        )
    query_grad, *kv_grads = filled
    mid_query_grad = contract_last(query_grad, query_raise).astype(low)
    mixture_arrived = shift(mixture_sent, 1)

    def kv_hop(k, arrived, dtype, *waits):
        return hop(origin(k), arrived, kv_grads, (tokens, kv_cols), dtype, waits)

    kv_sent = kv_hop(1, None, low, mixture_arrived)
    normed_query_grad = project(query_grad, query_weight, mid_query_grad, down_input[:rank], True, wide, (kv_sent,))
    for k in range(2, col_count):
        kv_sent = kv_hop(k, shift(kv_sent, 1), low, normed_query_grad)
        if k == 2:
            kv_second = kv_sent
    kv_own = kv_hop(col_count, shift(kv_sent, 1), wide)
    for k in range(3, col_count):
        last = k == col_count - 1
        mixture_sent = mixture_hop(k + 1, mixture_arrived, wide if last else low)
        mixture_arrived = None if last else shift(mixture_sent, 1)
    moe_slice = mixture_sent
    resid_slice = lax.dynamic_slice_in_dim(resid_full, col_index * col_width, col_width, 1)
    layer_output = resid_slice.astype(wide) + moe_slice
    key_grad = keys_back(kv_own[:, :kv_cols])[0].astype(low)
    value_grad = kv_own[:, kv_cols:].astype(low)
    kv_proj_grad = jnp.concatenate([key_grad, value_grad], axis=1)
    mid_kv_grad = jnp.concatenate(
        [
            contract_last(key_grad, key_value_raise[0]),
            contract_last(value_grad, key_value_raise[1]),
        ],
        axis=1,
    ).astype(low)
    mid_grad = jnp.concatenate([mid_query_grad, mid_kv_grad], axis=1)
    normed_in_grad = (
        normed_query_grad
        + product(kv_proj_grad, key_value_weight)
        + product(mid_kv_grad, local_in)
    )
    input_grad_own = (resid_grad + norm_in_back(normed_in_grad)[0]).astype(low)
    def of_all(part):
        return tree_sum([part] + [shift(part, k) for k in range(1, col_count)])

    up_part = contract_leading(middle_output, branch_grad).astype(low).reshape(-1, group_cols)
    head_part = jnp.concatenate(
        [contract_leading(middle[:, :rank], query_grad), contract_leading(mid_out_grad, heads)]
    ).astype(low)

    def head_piece(c):
        piece = lax.dynamic_slice_in_dim(head_part, c * group_cols, group_cols, 1)
        return jnp.concatenate([piece, up_part])

    head_trees = lax.all_gather(summed(exchange(head_piece), (kv_second,)), "row", axis=0)
    slot_hot = (slots[None, :] == jnp.arange(adapters, dtype=jnp.int32)[:, None]).astype(low)
    up_trees = head_trees[:, 2 * rank :].reshape(-1, rank, width)
    head_own = head_trees[:, : 2 * rank]
    head_square = jnp.einsum("st,tij->sij", slot_hot, head_own, preferred_element_type=wide)
    head_square = jnp.full((1, HEAD_WIDTH), jnp.sum(head_square * head_square))
    head_square = of_all(head_square)[:, :1]
    wait = nought(head_square)
    pieces = exchange(lambda c: lax.dynamic_slice_in_dim(input_grad_own, c * col_width + wait, col_width, 1))
    input_grad = in_order(pieces, 0).astype(wide)

    kv_portion = jnp.concatenate(
        [
            contract_leading(middle[:, rank : 2 * rank], key_grad),
            contract_leading(middle[:, 2 * rank :], value_grad),
        ]
    )
    in_portion = contract_leading(mid_grad, normalized)
    last_part = of_all(jnp.concatenate([in_portion, kv_portion.reshape(-1, width)]).astype(low))
    last_trees = lax.all_gather(last_part.astype(low), "row", axis=0)
    row_start = row_index * row_width
    in_own = lax.dynamic_slice_in_dim(last_trees[:, : 3 * rank], row_start, row_width, 2)
    up_own = lax.dynamic_slice_in_dim(up_trees, row_start, row_width, 2)
    kv_own_trees = last_trees[:, 3 * rank :].reshape(-1, 2 * rank, kv_cols)

    def flip(array):
        return array.transpose(0, 2, 1)

    def rows_of(array):
        return array.reshape(adapters, 2 * rank, kv_cols)

    grad_norm, following = update(
        slots,
        head_square,
        (up_trees, last_trees),
        (head_own[:, :rank], head_own[:, rank:], up_own, in_own, kv_own_trees),
        (
            (adapter_query_up, query_first_moment, query_second_moment),
            tuple(map(flip, (adapter_output_down, output_down_first_moment, output_down_second_moment))),
            tuple(map(flip, (adapter_output_up, output_up_first_moment, output_up_second_moment))),
            tuple(map(flip, (adapter_input_down, input_first_moment, input_second_moment))),
            tuple(map(rows_of, (adapter_key_value_up, key_value_first_moment, key_value_second_moment))),
        ),
        (
            learning_rate_upper,
            learning_rate_output,
            learning_rate_upper,
            learning_rate_lower,
            learning_rate_upper,
        ),
    )
    query_following, down_following, up_following, input_following, key_value_following = following
    return (
        layer_output,
        input_grad,
        grad_norm.reshape(()),
        *map(flip, input_following),
        *query_following,
        *(a.reshape(adapter_key_value_up.shape) for a in key_value_following),
        *map(flip, down_following),
        *map(flip, up_following),
        moe_slice,
    )


def solution(mesh):
    return jax.shard_map(
        shards,
        mesh=mesh,
        in_specs=(
            P("row", "col"),
            P("row", "col"),
            P(),
            P(),
            P(),
            P(),
            P("row", "col"),
            P("row", None),
            P("row", None),
            P("col", "row"),
            P("row", None),
            P("col", "row", None),
            P("col", None, "row"),
            P(None, "row", None),
            P(None, None, "col"),
            P(),
            P(None, "col", None),
            P(None, "row", None),
            P(None, "row", None),
            P(None, "row", None),
            P(None, None, "col"),
            P(None, None, "col"),
            P(),
            P(),
            P(None, "col", None),
            P(None, "col", None),
            P(None, "row", None),
            P(None, "row", None),
            P("row", None),
            P("row"),
            P("row", None),
            P("row", None),
        ),
        out_specs=(
            P("row", "col"),
            P("row", "col"),
            P(),
            P(None, "row", None),
            P(None, "row", None),
            P(None, "row", None),
            P(None, None, "col"),
            P(None, None, "col"),
            P(None, None, "col"),
            P(),
            P(),
            P(),
            P(None, "col", None),
            P(None, "col", None),
            P(None, "col", None),
            P(None, "row", None),
            P(None, "row", None),
            P(None, "row", None),
            P("row", "col"),
        ),
        check_vma=False,
    )
```

```python
import functools

import jax
import jax.numpy as jnp
from jax import lax
from jax.experimental import pallas as pl
from jax.experimental.pallas import tpu as pltpu
from jax.sharding import PartitionSpec as P

HEAD_WIDTH = 128
STEP = 10


norm_eps = 1e-06
rope_base = 1000000.0
beta_first = 0.9
beta_second = 0.999
adam_eps = 1e-08
decay_rate = 0.01
learning_rate_lower = 0.02
learning_rate_upper = 0.1
learning_rate_output = 0.25
clip_limit = 1.0
masked_score = -1e30
score_scale = HEAD_WIDTH ** (-0.5)
low = jnp.bfloat16
wide = jnp.float32


def contract_last(left, right):
    return lax.dot_general(left, right, (((1,), (1,)), ((), ())), preferred_element_type=wide)


def contract_leading(left, right):
    return lax.dot_general(left, right, (((0,), (0,)), ((), ())), preferred_element_type=wide)


def product(left, right):
    return jnp.dot(left, right, preferred_element_type=wide)


def rms_norm(values, gain):
    return values * lax.rsqrt(jnp.mean(values * values, axis=-1, keepdims=True) + norm_eps) * gain


def moment_update(weight, first, second, grad, rate):
    first = beta_first * first + (1.0 - beta_first) * grad
    second = beta_second * second + (1.0 - beta_second) * grad * grad
    first_hat = first / (1.0 - beta_first**STEP)
    second_hat = second / (1.0 - beta_second**STEP)
    weight = weight - rate * (first_hat / (jnp.sqrt(second_hat) + adam_eps) + decay_rate * weight)
    return (weight, first, second)


def nought(values):
    return jnp.isnan(values[0, 0].astype(wide)).astype(jnp.int32)


def held(kernel, inputs, waits):
    def run(*refs):
        return kernel(*refs[:inputs], *refs[inputs + waits :])

    return run


anywhere = pl.BlockSpec(memory_space=pl.ANY)


def project_kernel(turned, left_ref, weight_ref, thin_ref, thin_weight_ref, out_ref):
    whole = contract_last if turned else product
    total = whole(left_ref[...], weight_ref[...]) + product(thin_ref[...], thin_weight_ref[...])
    out_ref[...] = total.astype(out_ref.dtype)


def project(left, weight, thin, thin_weight, turned, dtype, waits=()):
    tokens, depth = left.shape
    cols = weight.shape[0 if turned else 1]
    rank = thin.shape[1]
    block = 512 if depth <= 2048 else 256
    if turned:
        weight_spec = pl.BlockSpec((block, depth), lambda j: (j, 0))
    else:
        weight_spec = pl.BlockSpec((depth, block), lambda j: (0, j))
    return pl.pallas_call(
        held(functools.partial(project_kernel, turned), 4, len(waits)),
        grid=(cols // block,),
        in_specs=[
            pl.BlockSpec((tokens, depth), lambda j: (0, 0)),
            weight_spec,
            pl.BlockSpec((tokens, rank), lambda j: (0, 0)),
            pl.BlockSpec((rank, block), lambda j: (0, j)),
            *[anywhere] * len(waits),
        ],
        out_specs=pl.BlockSpec((tokens, block), lambda j: (0, j)),
        out_shape=jax.ShapeDtypeStruct((tokens, cols), dtype),
        compiler_params=pltpu.CompilerParams(vmem_limit_bytes=60 << 20),
        cost_estimate=pl.CostEstimate(flops=0, bytes_accessed=0, transcendentals=0),
        name="project",
    )(left, weight, thin, thin_weight, *waits)


def shift(values, step):
    count = lax.axis_size("col")
    pairs = [(i, (i + step) % count) for i in range(count)]
    return lax.ppermute(values, "col", pairs)


def ring_gather(values):
    parts = [values]
    for _ in range(lax.axis_size("col") - 1):
        parts.append(shift(parts[-1], 1))
    return parts


def origin(k):
    count = lax.axis_size("col")
    return lax.rem(lax.axis_index("col") + count - k, count)


def in_order(parts, axis, wait=0):
    size = parts[0].shape[axis]
    shape = list(parts[0].shape)
    shape[axis] = size * len(parts)
    out = jnp.zeros(shape, parts[0].dtype)
    for k, part in enumerate(parts):
        out = lax.dynamic_update_slice_in_dim(out, part, origin(k) * size + wait, axis)
    return out


def ring_scatter(part_of):
    count = lax.axis_size("col")
    total = part_of(origin(1))
    for k in range(1, count):
        total = shift(total.astype(low), 1).astype(wide) + part_of(origin(k + 1))
    return total


def exchange(piece_of):
    count = lax.axis_size("col")
    return [piece_of(origin(0))] + [shift(piece_of(origin(count - k)), k) for k in range(1, count)]


def tree_sum(parts):
    if len(parts) == 1:
        return parts[0].astype(wide)
    return tree_sum(parts[0::2]) + tree_sum(parts[1::2])


def hop_kernel(arrives, count, *refs):
    arrived, own, out_ref = refs[1 : 1 + arrives], refs[1 + arrives : 1 + arrives + count], refs[-1]
    start = 0
    for ref in own:
        span = pl.ds(start, ref.shape[1])
        total = ref[...].astype(wide)
        if arrives:
            total = total + arrived[0][:, span].astype(wide)
        out_ref[:, span] = total.astype(out_ref.dtype)
        start += ref.shape[1]


def hop(place, arrived, own, block, dtype, waits=()):
    rows, cols = block
    across = own[0].shape[1] != cols
    step = min(rows, 256 if across else 64)
    steps = rows // step
    total = cols * len(own)

    def whole(i, p):
        return (i, 0)

    def mine(i, p):
        return (i, p[0]) if across else (p[0] * steps + i, 0)

    arrivals = () if arrived is None else (arrived,)
    return pl.pallas_call(
        held(functools.partial(hop_kernel, len(arrivals), len(own)), 1 + len(arrivals) + len(own), len(waits)),
        grid_spec=pltpu.PrefetchScalarGridSpec(
            num_scalar_prefetch=1,
            grid=(steps,),
            in_specs=[pl.BlockSpec((step, total), whole)] * len(arrivals)
            + [pl.BlockSpec((step, cols), mine)] * len(own)
            + [anywhere] * len(waits),
            out_specs=pl.BlockSpec((step, total), whole),
        ),
        out_shape=jax.ShapeDtypeStruct((rows, total), dtype),
        compiler_params=pltpu.CompilerParams(vmem_limit_bytes=60 << 20),
        name="hop",
    )(place.reshape(1), *arrivals, *own, *waits)


def sum_kernel(*refs):
    refs[-1][...] = tree_sum([ref[...] for ref in refs[:-1]]).astype(refs[-1].dtype)


def summed(parts, waits):
    shape = parts[0].shape
    return pl.pallas_call(
        held(sum_kernel, len(parts), len(waits)),
        grid=(1,),
        in_specs=[pl.BlockSpec(shape, lambda i: (0, 0))] * len(parts) + [anywhere] * len(waits),
        out_specs=pl.BlockSpec(shape, lambda i: (0, 0)),
        out_shape=jax.ShapeDtypeStruct(shape, parts[0].dtype),
        compiler_params=pltpu.CompilerParams(vmem_limit_bytes=60 << 20),
        name="summed",
    )(*parts, *waits)


def cut_kernel(place_ref, *refs):
    half = len(refs) // 2
    for ref, out_ref in zip(refs[:half], refs[half:]):
        out_ref[...] = ref[...]


def cut_and_send(values, rows, waits):
    count = lax.axis_size("col")
    cols = values.shape[1]
    places = [origin(0)] + [origin(count - k) for k in range(1, count)]

    def block(k):
        return pl.BlockSpec((rows, cols), lambda i, p: (p[k], 0))

    pieces = pl.pallas_call(
        held(cut_kernel, 1 + count, len(waits)),
        grid_spec=pltpu.PrefetchScalarGridSpec(
            num_scalar_prefetch=1,
            grid=(1,),
            in_specs=[block(k) for k in range(count)] + [anywhere] * len(waits),
            out_specs=[pl.BlockSpec((rows, cols), lambda i, p: (0, 0))] * count,
        ),
        out_shape=[jax.ShapeDtypeStruct((rows, cols), values.dtype)] * count,
        compiler_params=pltpu.CompilerParams(vmem_limit_bytes=60 << 20),
        name="cut",
    )(jnp.stack(places), *[values] * count, *waits)
    return [pieces[0]] + [shift(pieces[k], k) for k in range(1, count)]


def narrow_kernel(left_ref, right_ref, out_ref):
    out_ref[...] = contract_last(left_ref[...], right_ref[...]).astype(low)


def narrow(left, right, waits):
    return pl.pallas_call(
        held(narrow_kernel, 2, len(waits)),
        grid=(1,),
        in_specs=[
            pl.BlockSpec(left.shape, lambda i: (0, 0)),
            pl.BlockSpec(right.shape, lambda i: (0, 0)),
            *[anywhere] * len(waits),
        ],
        out_specs=pl.BlockSpec((left.shape[0], right.shape[0]), lambda i: (0, 0)),
        out_shape=jax.ShapeDtypeStruct((left.shape[0], right.shape[0]), low),
        compiler_params=pltpu.CompilerParams(vmem_limit_bytes=60 << 20),
        name="narrow",
    )(left, right, *waits)


def portions_kernel(left_ref, grad_ref, middle_ref, heads_ref, out_ref):
    rank = left_ref.shape[1]
    out_ref[:rank] = contract_leading(left_ref[...], grad_ref[...]).astype(low)
    out_ref[rank:] = contract_leading(middle_ref[...], heads_ref[...]).astype(low)


def portions(left, grad, middle, heads, waits):
    tokens, cols = grad.shape
    rank, block = left.shape[1], 1024

    def whole(j):
        return (0, 0)

    def part(j):
        return (0, j)

    return pl.pallas_call(
        held(portions_kernel, 4, len(waits)),
        grid=(cols // block,),
        in_specs=[
            pl.BlockSpec((tokens, rank), whole),
            pl.BlockSpec((tokens, block), part),
            pl.BlockSpec((tokens, rank), whole),
            pl.BlockSpec((tokens, block), part),
            *[anywhere] * len(waits),
        ],
        out_specs=pl.BlockSpec((2 * rank, block), part),
        out_shape=jax.ShapeDtypeStruct((2 * rank, cols), low),
        compiler_params=pltpu.CompilerParams(vmem_limit_bytes=60 << 20),
        name="portions",
    )(left, grad, middle, heads, *waits)


def head_forward(proj, gain, cos, sin):
    inv = lax.rsqrt(jnp.mean(proj * proj, axis=-1, keepdims=True) + norm_eps)
    scaled = proj * inv * gain
    return scaled * cos + pltpu.roll(scaled, HEAD_WIDTH // 2, 1) * sin, inv


def attend_kernel(share, proj_ref, cos_ref, sin_ref, gain_ref, bias_ref, key_ref, value_ref,
                  out_ref, lse_ref, value_t):
    @pl.when(lax.rem(pl.program_id(0), share) == 0)
    def _():
        value_t[...] = value_ref[...].T

    query, _ = head_forward(proj_ref[...], gain_ref[...], cos_ref[...], sin_ref[...])
    scores = contract_last(key_ref[...], query.astype(low)) * score_scale + bias_ref[...]
    top = jnp.max(scores, axis=0, keepdims=True)
    probs = jnp.exp(scores - top)
    total = jnp.sum(probs, axis=0, keepdims=True)
    mixed = product(value_t[...], probs.astype(low)) / total
    out_ref[...] = mixed.T.astype(low)
    lse_ref[0] = top + jnp.log(total)


def attend_back_kernel(share, proj_ref, cos_ref, sin_ref, gain_ref, bias_ref, key_ref, value_ref,
                       lse_ref, grad_ref, out_ref, kv_grad_ref, key_t, key_sum, value_sum):
    @pl.when(lax.rem(pl.program_id(0), share) == 0)
    def _():
        key_t[...] = key_ref[...].T
        key_sum[...] = jnp.zeros_like(key_sum)
        value_sum[...] = jnp.zeros_like(value_sum)

    proj, gain, cos, sin = proj_ref[...], gain_ref[...], cos_ref[...], sin_ref[...]
    query, inv = head_forward(proj, gain, cos, sin)
    query = query.astype(low)
    grad = grad_ref[...]
    scores = contract_last(key_ref[...], query) * score_scale + bias_ref[...]
    probs = jnp.exp(scores - lse_ref[0])
    probs_grad = contract_last(value_ref[...], grad)
    delta = jnp.sum(probs * probs_grad, axis=0, keepdims=True)
    scores_grad = (probs * (probs_grad - delta)).astype(low)
    value_sum[...] += product(probs.astype(low), grad)
    key_sum[...] += product(scores_grad, query)
    rotated = product(key_t[...], scores_grad).T * score_scale
    scaled = rotated * cos + pltpu.roll(rotated * sin, HEAD_WIDTH // 2, 1)
    scaled = scaled * gain
    slope = jnp.mean(scaled * proj, axis=-1, keepdims=True)
    out_ref[...] = (inv * scaled - proj * (inv * inv * inv * slope)).astype(low)

    @pl.when(lax.rem(pl.program_id(0), share) == share - 1)
    def _():
        kv_grad_ref[:, :HEAD_WIDTH] = (key_sum[...] * score_scale).astype(low)
        kv_grad_ref[:, HEAD_WIDTH:] = value_sum[...].astype(low)


def head_specs(tokens, length, first, share, kv_total):
    def head(h):
        return (0, first + h)

    def fixed(h):
        return (0, 0)

    return [
        pl.BlockSpec((tokens, HEAD_WIDTH), head),
        pl.BlockSpec((tokens, HEAD_WIDTH), fixed),
        pl.BlockSpec((tokens, HEAD_WIDTH), fixed),
        pl.BlockSpec((1, HEAD_WIDTH), fixed),
        pl.BlockSpec((length, tokens), fixed),
        pl.BlockSpec((length, HEAD_WIDTH), lambda h: (0, (first + h) // share)),
        pl.BlockSpec((length, HEAD_WIDTH), lambda h: (0, kv_total + (first + h) // share)),
    ]


def attend_cost(products, tokens, length, heads):
    return pl.CostEstimate(
        flops=4 * products * tokens * length * heads * HEAD_WIDTH,
        bytes_accessed=8 * tokens * heads * HEAD_WIDTH,
        transcendentals=tokens * length * heads,
    )


def attend(proj, cos, sin, gain, bias, keys_values):
    tokens, cols = proj.shape
    length, heads = keys_values.shape[0], cols // HEAD_WIDTH
    kv_total = keys_values.shape[1] // (2 * HEAD_WIDTH)
    share = heads // kv_total
    return pl.pallas_call(
        functools.partial(attend_kernel, share),
        grid=(heads,),
        in_specs=head_specs(tokens, length, 0, share, kv_total),
        out_specs=[
            pl.BlockSpec((tokens, HEAD_WIDTH), lambda h: (0, h)),
            pl.BlockSpec((1, 1, tokens), lambda h: (h, 0, 0)),
        ],
        scratch_shapes=[pltpu.VMEM((HEAD_WIDTH, length), low)],
        out_shape=[
            jax.ShapeDtypeStruct((tokens, cols), low),
            jax.ShapeDtypeStruct((heads, 1, tokens), wide),
        ],
        compiler_params=pltpu.CompilerParams(vmem_limit_bytes=60 << 20),
        cost_estimate=attend_cost(3, tokens, length, heads),
        name="attend",
    )(proj, cos, sin, gain, bias, keys_values, keys_values)


def attend_back(first, heads, proj, cos, sin, gain, bias, keys_values, lse, grad, kv_span, filled, waits):
    tokens, length = proj.shape[0], keys_values.shape[0]
    total = proj.shape[1] // HEAD_WIDTH
    kv_total = keys_values.shape[1] // (2 * HEAD_WIDTH)
    share = total // kv_total
    kv_first, kv_end = kv_span

    def head(h):
        return (0, first + h)

    return pl.pallas_call(
        held(functools.partial(attend_back_kernel, share), 9, len(filled) + len(waits)),
        grid=(heads,),
        in_specs=head_specs(tokens, length, first, share, kv_total)
        + [
            pl.BlockSpec((1, 1, tokens), lambda h: (first + h, 0, 0)),
            pl.BlockSpec((tokens, HEAD_WIDTH), head),
            *[anywhere] * (len(filled) + len(waits)),
        ],
        out_specs=[
            pl.BlockSpec((tokens, HEAD_WIDTH), head),
            pl.BlockSpec((length, 2 * HEAD_WIDTH), lambda h: (0, (first + h) // share - kv_first)),
        ],
        scratch_shapes=[
            pltpu.VMEM((HEAD_WIDTH, length), low),
            pltpu.VMEM((length, HEAD_WIDTH), wide),
            pltpu.VMEM((length, HEAD_WIDTH), wide),
        ],
        out_shape=[
            jax.ShapeDtypeStruct(proj.shape, low),
            jax.ShapeDtypeStruct((length, (kv_end - kv_first) * 2 * HEAD_WIDTH), low),
        ],
        input_output_aliases={9 + i: i for i in range(len(filled))},
        compiler_params=pltpu.CompilerParams(vmem_limit_bytes=60 << 20),
        cost_estimate=pl.CostEstimate(flops=0, bytes_accessed=0, transcendentals=0),
        name="attend_back",
    )(proj, cos, sin, gain, bias, keys_values, keys_values, lse, grad, *filled, *waits)


def experts_kernel(place_ref, normed_ref, back_ref, weight_ref, gate_ref, up_ref, down_ref,
                   post_ref, out_ref, out_sum):
    e = pl.program_id(0)
    width = normed_ref.shape[1]

    @pl.when(e == 0)
    def _():
        post_ref[...] = jnp.zeros_like(post_ref)
        out_sum[...] = jnp.zeros_like(out_sum)

    normed = normed_ref[...]
    gate = product(normed, gate_ref[0])
    up = product(normed, up_ref[0])
    back = back_ref[...]
    weights = weight_ref[...]
    lane = lax.broadcasted_iota(jnp.int32, weights.shape, 1)
    weight = jnp.sum(jnp.where(lane == e, weights, 0.0), axis=1, keepdims=True)
    sig = jax.nn.sigmoid(gate)
    act = gate * sig
    inner = act * up
    lane = lax.broadcasted_iota(jnp.int32, (normed.shape[0], HEAD_WIDTH), 1)
    gate_sum = jnp.sum(inner * back, axis=1, keepdims=True)
    post_ref[:, width:] += jnp.where(lane == place_ref[1] + e, gate_sum, 0.0)
    back = back * weight
    gate_grad = (back * up * (sig + act * (1.0 - sig))).astype(low)
    up_grad = (back * act).astype(low)
    out_sum[...] += product((inner * weight).astype(low), down_ref[...])
    post_ref[:, :width] += contract_last(gate_grad, gate_ref[0]) + contract_last(up_grad, up_ref[0])

    @pl.when(e == pl.num_programs(0) - 1)
    def _():
        out_ref[...] = out_sum[...].astype(low)


def experts(chunk, first_expert, tokens, normed, back, weights, gate_up, down, mixture, waits):
    filled = () if mixture is None else (mixture,)
    waits = (*filled, *waits)
    width = normed.shape[1]
    count, inner_width = gate_up.shape[0], gate_up.shape[2] // 2
    return pl.pallas_call(
        held(experts_kernel, 7, len(waits)),
        grid_spec=pltpu.PrefetchScalarGridSpec(
            num_scalar_prefetch=1,
            grid=(count,),
            in_specs=[
                pl.BlockSpec((tokens, width), lambda e, p: (p[0], 0)),
                pl.BlockSpec((tokens, inner_width), lambda e, p: (p[0], e)),
                pl.BlockSpec((tokens, count), lambda e, p: (p[0], 0)),
                pl.BlockSpec((1, width, inner_width), lambda e, p: (e, 0, 0)),
                pl.BlockSpec((1, width, inner_width), lambda e, p: (e, 0, 1)),
                pl.BlockSpec((inner_width, width), lambda e, p: (e, 0)),
                *[anywhere] * len(waits),
            ],
            out_specs=[
                pl.BlockSpec((tokens, width + HEAD_WIDTH), lambda e, p: (0, 0)),
                pl.BlockSpec((tokens, width), lambda e, p: (p[0], 0)),
            ],
            scratch_shapes=[pltpu.VMEM((tokens, width), wide)],
        ),
        out_shape=[
            jax.ShapeDtypeStruct((tokens, width + HEAD_WIDTH), wide),
            jax.ShapeDtypeStruct(normed.shape, low),
        ],
        input_output_aliases={7: 1} if filled else {},
        compiler_params=pltpu.CompilerParams(vmem_limit_bytes=60 << 20),
        cost_estimate=pl.CostEstimate(
            flops=10 * tokens * width * count * inner_width,
            bytes_accessed=6 * width * count * inner_width,
            transcendentals=tokens * count * inner_width,
        ),
        name="experts",
    )(jnp.stack([chunk, first_expert]), normed, back, weights, gate_up, gate_up, down, *waits)


def settle_kernel(arrived_ref, post_ref, probs_ref, router_ref, resid_ref, gain_ref, cot_ref, up_ref,
                  grad_ref, branch_ref, middle_ref):
    width = resid_ref.shape[1]
    gate_grad = arrived_ref[:, width:].astype(wide) + post_ref[:, width:]
    probs = probs_ref[...]
    logits_grad = probs * (gate_grad - jnp.sum(probs * gate_grad, axis=1, keepdims=True))
    grad = arrived_ref[:, :width].astype(wide) + post_ref[:, :width]
    grad = (grad + product(logits_grad.astype(low), router_ref[...])) * gain_ref[...]
    resid = resid_ref[...]
    inv = lax.rsqrt(jnp.mean(resid * resid, axis=1, keepdims=True) + norm_eps)
    slope = jnp.mean(grad * resid, axis=1, keepdims=True)
    grad = cot_ref[...].astype(wide) + inv * grad - resid * (inv * inv * inv * slope)
    grad_ref[...] = grad
    branch = grad.astype(low)
    branch_ref[...] = branch
    middle_ref[...] = contract_last(branch, up_ref[...]).astype(low)


def settle(arrived, post, probs, router, resid, gain, cot, up):
    tokens, width = resid.shape
    rank = up.shape[0]
    block = min(tokens, 64)
    lanes = arrived.shape[1] - width

    def rows(cols):
        return pl.BlockSpec((block, cols), lambda i: (i, 0))

    def whole(*shape):
        return pl.BlockSpec(shape, lambda i: (0, 0))

    return pl.pallas_call(
        settle_kernel,
        grid=(tokens // block,),
        in_specs=[
            rows(width + lanes),
            rows(width + lanes),
            rows(lanes),
            whole(lanes, width),
            rows(width),
            whole(1, width),
            rows(width),
            whole(rank, width),
        ],
        out_specs=[rows(width), rows(width), rows(rank)],
        out_shape=[
            jax.ShapeDtypeStruct((tokens, width), wide),
            jax.ShapeDtypeStruct((tokens, width), low),
            jax.ShapeDtypeStruct((tokens, rank), low),
        ],
        compiler_params=pltpu.CompilerParams(vmem_limit_bytes=60 << 20),
        cost_estimate=pl.CostEstimate(flops=0, bytes_accessed=0, transcendentals=0),
        name="settle",
    )(arrived, post, probs, router, resid, gain, cot, up)


def update_kernel(rates, rank, row_width, slot_ref, place_ref, square_ref, head_ref, last_ref, *refs):
    size = 3 * len(rates)
    state, norm_ref, outs = refs[:size], refs[size], refs[size + 1 : 2 * size + 1]
    head_sum, last_sum, factor_ref = refs[2 * size + 1 :]
    now = pl.program_id(0)

    @pl.when(now == 0)
    def _():
        head_sum[...] = jnp.zeros_like(head_sum)
        last_sum[...] = jnp.zeros_like(last_sum)

        def tree(t, carry):
            at = slot_ref[t]
            head_sum[at] += head_ref[t].astype(wide)
            last_sum[at] += last_ref[t].astype(wide)
            return carry

        lax.fori_loop(0, head_ref.shape[0], tree, 0)

        def square(s, carry):
            head, last = head_sum[s, 2 * rank :], last_sum[s]
            head = jnp.sum(head * head, axis=0, keepdims=True)
            last = jnp.sum(last * last, axis=0, keepdims=True)
            return carry + jnp.sum(head, axis=1, keepdims=True) + jnp.sum(last, axis=1, keepdims=True)

        norm = jnp.sqrt(lax.fori_loop(0, head_sum.shape[0], square, square_ref[...]))
        norm_ref[...] = norm
        factor_ref[...] = jnp.minimum(1.0, clip_limit / (norm + 1e-06))

    chunk = pl.multiple_of(2 * rank * (1 + place_ref[0]), 2 * rank)
    inside = pl.ds(pl.multiple_of(place_ref[1], HEAD_WIDTH), row_width)
    across = pl.ds(pl.multiple_of(place_ref[2], HEAD_WIDTH), row_width)
    up = head_sum[now, pl.ds(chunk, rank), inside]
    query_in = head_sum[now, pl.ds(chunk + rank, rank), inside]
    kv_in = last_sum[now, : 2 * rank, across]
    kv = last_sum[now, 2 * rank :, :]
    kv_cols = state[-1].shape[2]
    grads = (
        head_sum[now, :rank, :],
        head_sum[now, rank : 2 * rank, :],
        up,
        jnp.concatenate([query_in, kv_in], axis=0),
        jnp.concatenate([kv[:, i : i + kv_cols] for i in range(0, kv.shape[1], kv_cols)], axis=0),
    )
    factor = factor_ref[...]
    for i, (grad, rate) in enumerate(zip(grads, rates)):
        weight, first, second = (ref[0] for ref in state[3 * i : 3 * i + 3])
        new = moment_update(weight, first, second, grad * factor, rate)
        for ref, value in zip(outs[3 * i : 3 * i + 3], new):
            ref[0] = value


def update(slots, place, square, head_trees, last_trees, states, rates, rank, row_width):
    state = [array for triple in states for array in triple]
    adapters = state[0].shape[0]

    def all_of(array):
        return pl.BlockSpec(array.shape, lambda s: (0,) * array.ndim)

    def one_of(array):
        return pl.BlockSpec((1, *array.shape[1:]), lambda s: (s, 0, 0))

    out = pl.pallas_call(
        functools.partial(update_kernel, tuple(rates), rank, row_width),
        grid=(adapters,),
        in_specs=[pl.BlockSpec(memory_space=pltpu.SMEM)] * 2
        + [all_of(a) for a in (square, head_trees, last_trees)]
        + [one_of(a) for a in state],
        out_specs=[all_of(square)] + [one_of(a) for a in state],
        out_shape=[jax.ShapeDtypeStruct((1, 1), wide)]
        + [jax.ShapeDtypeStruct(a.shape, wide) for a in state],
        scratch_shapes=[
            pltpu.VMEM((adapters, *head_trees.shape[1:]), wide),
            pltpu.VMEM((adapters, *last_trees.shape[1:]), wide),
            pltpu.VMEM((1, 1), wide),
        ],
        compiler_params=pltpu.CompilerParams(vmem_limit_bytes=60 << 20),
        name="update",
    )(slots, place, square, head_trees, last_trees, *state)
    return out[0], [out[1 + 3 * i : 4 + 3 * i] for i in range(len(states))]


def tree_layout(lengths, parents, token_count, first, count):
    nodes = lengths.shape[0]
    node_ids = jnp.arange(nodes, dtype=jnp.int32)
    node_ends = jnp.cumsum(lengths, dtype=jnp.int32)
    node_starts = node_ends - lengths
    parent_hot = parents[:, None] == node_ids[None, :]
    eye = node_ids[:, None] == node_ids[None, :]
    grand_hot = jnp.any(parent_hot[:, :, None] & parent_hot[None, :, :], axis=1)
    ancestor = eye | parent_hot | grand_hot
    before = jnp.sum(jnp.where(ancestor & ~eye, lengths[None, :], 0), axis=1, dtype=jnp.int32)

    def hot_of(tokens):
        return (tokens[:, None] >= node_starts[None, :]) & (tokens[:, None] < node_ends[None, :])

    keys = jnp.arange(token_count, dtype=jnp.int32)
    queries = first + jnp.arange(count, dtype=jnp.int32)
    query_hot = hot_of(queries)
    positions = queries + jnp.sum(
        jnp.where(query_hot, (before - node_starts)[None, :], 0), axis=1, dtype=jnp.int32
    )
    reach = product(query_hot.astype(low), ancestor.astype(low)).astype(low)
    reachable = contract_last(hot_of(keys).astype(low), reach) > 0.5
    allowed = reachable & (keys[:, None] <= queries[None, :])
    return positions, jnp.where(allowed, 0.0, masked_score)


def shards(
    inputs,
    cotangent,
    attention_norm_gain,
    expert_norm_gain,
    query_norm_gain,
    key_norm_gain,
    frozen_query_weight,
    frozen_key_weight,
    frozen_value_weight,
    frozen_output_weight,
    frozen_router_weight,
    expert_gate_up_weight,
    expert_down_weight,
    adapter_input_down,
    adapter_query_up,
    adapter_key_value_up,
    adapter_output_down,
    adapter_output_up,
    input_first_moment,
    input_second_moment,
    query_first_moment,
    query_second_moment,
    key_value_first_moment,
    key_value_second_moment,
    output_down_first_moment,
    output_down_second_moment,
    output_up_first_moment,
    output_up_second_moment,
    routes,
    tree_adapter_index,
    tree_node_length,
    parents,
):
    col_count = lax.axis_size("col")
    row_count = lax.axis_size("row")
    col_index = lax.axis_index("col")
    row_index = lax.axis_index("row")
    length, col_width = inputs.shape
    width = col_width * col_count
    tokens = length // col_count
    first_token = col_index * tokens
    row_width = frozen_key_weight.shape[0]
    group_cols = frozen_query_weight.shape[1]
    kv_total = frozen_key_weight.shape[1] // HEAD_WIDTH
    kv_cols = kv_total * HEAD_WIDTH
    rank = adapter_query_up.shape[1]
    adapters = adapter_input_down.shape[0]
    local_experts = expert_gate_up_weight.shape[0]
    expert_total = frozen_router_weight.shape[1]
    inner_width = expert_down_weight.shape[1]
    slot = tree_adapter_index[0]

    def gather_rows(values, axis):
        return lax.all_gather(values, "row", axis=axis, tiled=True)

    local_inner = local_experts * inner_width
    first = gather_rows(
        jnp.concatenate(
            [
                expert_down_weight.reshape(local_inner, row_width),
                adapter_input_down.transpose(0, 2, 1).reshape(-1, row_width).astype(low),
                adapter_output_up.transpose(0, 2, 1).reshape(-1, row_width).astype(low),
                frozen_router_weight.T,
                jnp.broadcast_to(slot.astype(low), (16, row_width)),
                frozen_key_weight.T,
                frozen_value_weight.T,
            ]
        ),
        1,
    )
    in_start = local_inner
    up_start = in_start + adapters * 3 * rank
    router_start = up_start + adapters * rank
    slot_start = router_start + expert_total
    kv_start = slot_start + 16
    down_input = lax.dynamic_slice_in_dim(first, in_start + slot * 3 * rank, 3 * rank, 0)
    up_output = lax.dynamic_slice_in_dim(first, up_start + slot * rank, rank, 0)
    router = first[router_start:slot_start]
    slots = first[slot_start, ::row_width].astype(jnp.int32)
    key_value_weight = first[kv_start:]
    query_weight = gather_rows(in_order(ring_gather(frozen_query_weight), 1), 0)
    out_weight = gather_rows(in_order(ring_gather(frozen_output_weight), 0), 1)
    gate_up_weight = gather_rows(expert_gate_up_weight, 1)
    head_adapters = in_order(
        ring_gather(
            jnp.concatenate([adapter_query_up[slot], adapter_output_down[slot].T]).astype(low)
        ),
        1,
    )
    query_raise = head_adapters[:rank]
    down_output = head_adapters[rank:]
    key_value_raise = adapter_key_value_up[slot].astype(low)

    pieces = exchange(lambda c: lax.dynamic_slice_in_dim(inputs, c * tokens, tokens, 0))
    hidden_input = in_order(pieces, 1).astype(wide)
    cot_full = in_order(ring_gather(cotangent), 1)
    cot_own = lax.dynamic_slice_in_dim(cot_full, first_token, tokens, 0)
    positions, bias = tree_layout(tree_node_length[0], parents[0], length, first_token, tokens)

    def norm_in(values):
        return rms_norm(values, attention_norm_gain)

    normalized, norm_in_back = jax.vjp(norm_in, hidden_input)
    normalized = normalized.astype(low)
    middle = contract_last(normalized, down_input).astype(low)
    half = HEAD_WIDTH // 2
    frequency = rope_base ** (-jnp.arange(half, dtype=wide) / half)
    angles = positions.astype(wide)[:, None] * frequency[None, :]
    cos = jnp.concatenate([jnp.cos(angles)] * 2, axis=1)
    sin = jnp.concatenate([-jnp.sin(angles), jnp.sin(angles)], axis=1)

    def shape_keys(proj):
        parts = []
        for head in range(kv_total):
            scaled = rms_norm(proj[:, head * HEAD_WIDTH : (head + 1) * HEAD_WIDTH], key_norm_gain)
            turned = jnp.concatenate([scaled[:, half:], scaled[:, :half]], axis=1)
            parts.append(scaled * cos + turned * sin)
        return jnp.concatenate(parts, axis=1)

    key_value_proj = contract_last(normalized, key_value_weight)
    key_proj = key_value_proj[:, :kv_cols] + product(middle[:, rank : 2 * rank], key_value_raise[0])
    value_proj = key_value_proj[:, kv_cols:] + product(middle[:, 2 * rank :], key_value_raise[1])
    key_rot, keys_back = jax.vjp(shape_keys, key_proj)
    keys_values = in_order(
        ring_gather(jnp.concatenate([key_rot.astype(low), value_proj.astype(low)], axis=1)), 0
    )
    query_gain = query_norm_gain[None, :]
    proj = project(normalized, query_weight, middle[:, :rank], query_raise, False, wide)
    heads, totals = attend(proj, cos, sin, query_gain, bias, keys_values)
    inner_back = contract_last(cot_full, first[:local_inner])
    middle_output = contract_last(heads, down_output).astype(low)
    resid = hidden_input + project(
        heads, out_weight, middle_output, up_output, False, wide, (inner_back,)
    )

    resid_full = in_order(ring_gather(resid.astype(low)), 0)
    normed_post = rms_norm(resid_full.astype(wide), expert_norm_gain).astype(low)
    logits = contract_last(normed_post, router)
    expert_ids = jnp.arange(expert_total, dtype=jnp.int32)
    chosen = jnp.any(routes[:, :, None] == expert_ids[None, None, :], axis=1)
    shifted = logits - jnp.max(jnp.where(chosen, logits, -jnp.inf), axis=1, keepdims=True)
    raised = jnp.where(chosen, jnp.exp(jnp.where(chosen, shifted, 0.0)), 0.0)
    gate_probs = raised / jnp.sum(raised, axis=1, keepdims=True)
    local_probs = lax.dynamic_slice_in_dim(gate_probs, col_index * local_experts, local_experts, 1)
    own_probs = jnp.pad(
        lax.dynamic_slice_in_dim(gate_probs, first_token, tokens, 0),
        ((0, 0), (0, HEAD_WIDTH - expert_total)),
    )
    router_rows = jnp.pad(router, ((0, HEAD_WIDTH - expert_total), (0, 0)))
    local_in = down_input[rank:]
    mixture, arrived, sent = None, None, ()
    for k in range(col_count):
        post, mixture = experts(
            origin(k + 1),
            col_index * local_experts,
            tokens,
            normed_post,
            inner_back,
            local_probs,
            gate_up_weight,
            first,
            mixture,
            sent if k < col_count - 1 else (*sent, own_probs, router_rows, cot_own, local_in),
        )
        if k < col_count - 1:
            sent = ((post if k == 0 else arrived.astype(wide) + post).astype(low),)
            arrived = shift(sent[0], 1)

    def mixture_hop(k, arrived, dtype, *waits):
        return hop(origin(k), arrived, (mixture,), (length, col_width), dtype, waits)

    resid_grad, branch_grad, mid_out_grad = settle(
        arrived, post, own_probs, router_rows, resid, expert_norm_gain[None, :], cot_own, up_output
    )
    mixture_sent = mixture_hop(1, None, low, arrived)
    heads_grad = project(branch_grad, out_weight, mid_out_grad, down_output, True, low)
    head_count = proj.shape[1] // HEAD_WIDTH

    def heads_back(first, count, kv_span, filled, *waits):
        return attend_back(
            first * head_count // 4,
            count * head_count // 4,
            proj,
            cos,
            sin,
            query_gain,
            bias,
            keys_values,
            totals,
            heads_grad,
            kv_span,
            filled,
            waits,
        )

    filled = heads_back(0, 1, (0, kv_total // 2), ())
    mixture_sent = mixture_hop(2, shift(mixture_sent, 1), low, filled[0])
    query_grad, kv_grad = heads_back(1, 1, (0, kv_total // 2), filled, mixture_sent)
    pieces = cut_and_send(kv_grad, tokens, ())
    mixture_arrived = shift(mixture_sent, 1)
    query_grad, kv_grad = heads_back(2, 2, (kv_total // 2, kv_total), (query_grad,))
    kv_own = [summed(pieces, (query_grad, mixture_arrived)), None]
    pieces = cut_and_send(kv_grad, tokens, (kv_own[0],))
    mid_query_grad = narrow(query_grad, query_raise, (pieces[0],))
    head_part = portions(middle[:, :rank], query_grad, mid_out_grad, heads, (pieces[0],))
    normed_query_grad = project(
        query_grad, query_weight, mid_query_grad, down_input[:rank], True, wide, (head_part,)
    )
    kv_own[1] = tree_sum(pieces)
    kv_own = jnp.concatenate([half.astype(wide) for half in kv_own], axis=1)
    kv_split = [kv_own[:, i : i + HEAD_WIDTH] for i in range(0, 2 * kv_cols, HEAD_WIDTH)]
    key_grad = keys_back(jnp.concatenate(kv_split[0::2], axis=1))[0].astype(low)
    value_grad = jnp.concatenate(kv_split[1::2], axis=1).astype(low)
    kv_proj_grad = jnp.concatenate([key_grad, value_grad], axis=1)
    mid_kv_grad = jnp.concatenate(
        [
            contract_last(key_grad, key_value_raise[0]),
            contract_last(value_grad, key_value_raise[1]),
        ],
        axis=1,
    ).astype(low)

    def folded(part, cols):
        return jnp.concatenate([part[:, i : i + cols] for i in range(0, part.shape[1], cols)])

    early_part = jnp.concatenate(
        [contract_leading(middle_output, branch_grad), contract_leading(mid_query_grad, normalized)]
    ).astype(low)
    early_part = folded(early_part, group_cols)
    def head_piece(c):
        piece = lax.dynamic_slice_in_dim(head_part, c * group_cols, group_cols, 1)
        return jnp.concatenate([piece, early_part])

    kv_portion = jnp.concatenate(
        [
            contract_leading(middle[:, rank : 2 * rank], key_grad),
            contract_leading(middle[:, 2 * rank :], value_grad),
        ]
    )
    kv_rows = 2 * rank * kv_cols // width
    kv_portion = jnp.concatenate(
        [kv_portion[i : i + kv_rows] for i in range(0, 2 * rank, kv_rows)], axis=1
    )
    last_part = jnp.concatenate([contract_leading(mid_kv_grad, normalized), kv_portion]).astype(low)
    last_pieces = [last_part] + [shift(last_part, k) for k in range(1, col_count)]
    last_trees = lax.all_gather(tree_sum(last_pieces).astype(low), "row", axis=0)
    head_trees = lax.all_gather(summed(exchange(head_piece), ()), "row", axis=0)
    slot_hot = (slots[None, :] == jnp.arange(adapters, dtype=jnp.int32)[:, None]).astype(low)
    head_square = jnp.einsum(
        "st,tij->sij", slot_hot, head_trees[:, : 2 * rank], preferred_element_type=wide
    )
    head_square = jnp.full((1, HEAD_WIDTH), jnp.sum(head_square * head_square))
    head_square = tree_sum([head_square] + [shift(head_square, k) for k in range(1, col_count)])[:, :1]
    wait = nought(head_square)

    normed_in_grad = (
        normed_query_grad
        + product(kv_proj_grad, key_value_weight)
        + product(mid_kv_grad, local_in)
    )
    input_grad_own = (resid_grad + norm_in_back(normed_in_grad)[0]).astype(low)
    pieces = exchange(
        lambda c: lax.dynamic_slice_in_dim(input_grad_own, c * col_width + wait, col_width, 1)
    )
    input_grad = in_order(pieces, 0).astype(wide)
    for k in range(2, col_count):
        last = k == col_count - 1
        waits = (last_part,) if k == 2 else ()
        mixture_sent = mixture_hop(k + 1, mixture_arrived, wide if last else low, *waits)
        mixture_arrived = None if last else shift(mixture_sent, 1)
    moe_slice = mixture_sent
    resid_slice = lax.dynamic_slice_in_dim(resid_full, col_index * col_width, col_width, 1)
    layer_output = resid_slice.astype(wide) + moe_slice

    def flip(array):
        return array.transpose(0, 2, 1)

    def rows_of(array):
        return array.reshape(adapters, 2 * rank, kv_cols)

    row_start = row_index * row_width
    place = jnp.stack([row_start // group_cols, lax.rem(row_start, group_cols), row_start])
    grad_norm, following = update(
        slots,
        place,
        head_square,
        head_trees,
        last_trees,
        (
            (adapter_query_up, query_first_moment, query_second_moment),
            tuple(map(flip, (adapter_output_down, output_down_first_moment, output_down_second_moment))),
            tuple(map(flip, (adapter_output_up, output_up_first_moment, output_up_second_moment))),
            tuple(map(flip, (adapter_input_down, input_first_moment, input_second_moment))),
            tuple(map(rows_of, (adapter_key_value_up, key_value_first_moment, key_value_second_moment))),
        ),
        (
            learning_rate_upper,
            learning_rate_output,
            learning_rate_upper,
            learning_rate_lower,
            learning_rate_upper,
        ),
        rank,
        row_width,
    )
    query_following, down_following, up_following, input_following, key_value_following = following
    return (
        layer_output,
        input_grad,
        grad_norm.reshape(()),
        *map(flip, input_following),
        *query_following,
        *(a.reshape(adapter_key_value_up.shape) for a in key_value_following),
        *map(flip, down_following),
        *map(flip, up_following),
        moe_slice,
    )


def solution(mesh):
    return jax.shard_map(
        shards,
        mesh=mesh,
        in_specs=(
            P("row", "col"),
            P("row", "col"),
            P(),
            P(),
            P(),
            P(),
            P("row", "col"),
            P("row", None),
            P("row", None),
            P("col", "row"),
            P("row", None),
            P("col", "row", None),
            P("col", None, "row"),
            P(None, "row", None),
            P(None, None, "col"),
            P(),
            P(None, "col", None),
            P(None, "row", None),
            P(None, "row", None),
            P(None, "row", None),
            P(None, None, "col"),
            P(None, None, "col"),
            P(),
            P(),
            P(None, "col", None),
            P(None, "col", None),
            P(None, "row", None),
            P(None, "row", None),
            P("row", None),
            P("row"),
            P("row", None),
            P("row", None),
        ),
        out_specs=(
            P("row", "col"),
            P("row", "col"),
            P(),
            P(None, "row", None),
            P(None, "row", None),
            P(None, "row", None),
            P(None, None, "col"),
            P(None, None, "col"),
            P(None, None, "col"),
            P(),
            P(),
            P(),
            P(None, "col", None),
            P(None, "col", None),
            P(None, "col", None),
            P(None, "row", None),
            P(None, "row", None),
            P(None, "row", None),
            P("row", "col"),
        ),
        check_vma=False,
    )
```

```python
import functools

import jax
import jax.numpy as jnp
from jax import lax
from jax.experimental import pallas as pl
from jax.experimental.pallas import tpu as pltpu
from jax.sharding import PartitionSpec as P

HEAD_WIDTH = 128
STEP = 10


norm_eps = 1e-06
rope_base = 1000000.0
beta_first = 0.9
beta_second = 0.999
adam_eps = 1e-08
decay_rate = 0.01
learning_rate_lower = 0.02
learning_rate_upper = 0.1
learning_rate_output = 0.25
clip_limit = 1.0
masked_score = -1e30
score_scale = HEAD_WIDTH ** (-0.5)
low = jnp.bfloat16
wide = jnp.float32


def contract_last(left, right):
    return lax.dot_general(left, right, (((1,), (1,)), ((), ())), preferred_element_type=wide)


def contract_leading(left, right):
    return lax.dot_general(left, right, (((0,), (0,)), ((), ())), preferred_element_type=wide)


def product(left, right):
    return jnp.dot(left, right, preferred_element_type=wide)


def rms_norm(values, gain):
    return values * lax.rsqrt(jnp.mean(values * values, axis=-1, keepdims=True) + norm_eps) * gain


def moment_update(weight, first, second, grad, rate):
    first = beta_first * first + (1.0 - beta_first) * grad
    second = beta_second * second + (1.0 - beta_second) * grad * grad
    first_hat = first / (1.0 - beta_first**STEP)
    second_hat = second / (1.0 - beta_second**STEP)
    weight = weight - rate * (first_hat / (jnp.sqrt(second_hat) + adam_eps) + decay_rate * weight)
    return (weight, first, second)


def nought(values):
    return jnp.isnan(values[0, 0].astype(wide)).astype(jnp.int32)


def held(kernel, inputs, waits):
    def run(*refs):
        return kernel(*refs[:inputs], *refs[inputs + waits :])

    return run


anywhere = pl.BlockSpec(memory_space=pl.ANY)


def project_kernel(turned, left_ref, weight_ref, *refs):
    whole = contract_last if turned else product
    total = whole(left_ref[...], weight_ref[...])
    if len(refs) > 1:
        total = total + product(refs[0][...], refs[1][...])
    refs[-1][...] = total.astype(refs[-1].dtype)


def project(left, weight, thins, turned, dtype, waits=()):
    tokens, depth = left.shape
    cols = weight.shape[0 if turned else 1]
    block = 512 if depth <= 2048 else 256
    if turned:
        weight_spec = pl.BlockSpec((block, depth), lambda j: (j, 0))
    else:
        weight_spec = pl.BlockSpec((depth, block), lambda j: (0, j))
    return pl.pallas_call(
        held(functools.partial(project_kernel, turned), 2 + len(thins), len(waits)),
        grid=(cols // block,),
        in_specs=[
            pl.BlockSpec((tokens, depth), lambda j: (0, 0)),
            weight_spec,
            *[pl.BlockSpec(a.shape, lambda j: (0, 0)) for a in thins[:1]],
            *[pl.BlockSpec((a.shape[0], block), lambda j: (0, j)) for a in thins[1:]],
            *[anywhere] * len(waits),
        ],
        out_specs=pl.BlockSpec((tokens, block), lambda j: (0, j)),
        out_shape=jax.ShapeDtypeStruct((tokens, cols), dtype),
        compiler_params=pltpu.CompilerParams(vmem_limit_bytes=60 << 20),
        cost_estimate=pl.CostEstimate(flops=0, bytes_accessed=0, transcendentals=0),
        name="project",
    )(left, weight, *thins, *waits)


def shift(values, step):
    count = lax.axis_size("col")
    pairs = [(i, (i + step) % count) for i in range(count)]
    return lax.ppermute(values, "col", pairs)


def ring_gather(values):
    parts = [values]
    for _ in range(lax.axis_size("col") - 1):
        parts.append(shift(parts[-1], 1))
    return parts


def origin(k):
    count = lax.axis_size("col")
    return lax.rem(lax.axis_index("col") + count - k, count)


def in_order(parts, axis, wait=0):
    size = parts[0].shape[axis]
    shape = list(parts[0].shape)
    shape[axis] = size * len(parts)
    out = jnp.zeros(shape, parts[0].dtype)
    for k, part in enumerate(parts):
        out = lax.dynamic_update_slice_in_dim(out, part, origin(k) * size + wait, axis)
    return out


def ring_scatter(part_of):
    count = lax.axis_size("col")
    total = part_of(origin(1))
    for k in range(1, count):
        total = shift(total.astype(low), 1).astype(wide) + part_of(origin(k + 1))
    return total


def exchange(piece_of):
    count = lax.axis_size("col")
    return [piece_of(origin(0))] + [shift(piece_of(origin(count - k)), k) for k in range(1, count)]


def tree_sum(parts):
    if len(parts) == 1:
        return parts[0].astype(wide)
    return tree_sum(parts[0::2]) + tree_sum(parts[1::2])


def hop_kernel(arrives, count, *refs):
    arrived, own, out_ref = refs[1 : 1 + arrives], refs[1 + arrives : 1 + arrives + count], refs[-1]
    start = 0
    for ref in own:
        span = pl.ds(start, ref.shape[1])
        total = ref[...].astype(wide)
        if arrives:
            total = total + arrived[0][:, span].astype(wide)
        out_ref[:, span] = total.astype(out_ref.dtype)
        start += ref.shape[1]


def hop(place, arrived, own, block, dtype, waits=()):
    rows, cols = block
    across = own[0].shape[1] != cols
    step = min(rows, 256 if across else 64)
    steps = rows // step
    total = cols * len(own)

    def whole(i, p):
        return (i, 0)

    def mine(i, p):
        return (i, p[0]) if across else (p[0] * steps + i, 0)

    arrivals = () if arrived is None else (arrived,)
    return pl.pallas_call(
        held(functools.partial(hop_kernel, len(arrivals), len(own)), 1 + len(arrivals) + len(own), len(waits)),
        grid_spec=pltpu.PrefetchScalarGridSpec(
            num_scalar_prefetch=1,
            grid=(steps,),
            in_specs=[pl.BlockSpec((step, total), whole)] * len(arrivals)
            + [pl.BlockSpec((step, cols), mine)] * len(own)
            + [anywhere] * len(waits),
            out_specs=pl.BlockSpec((step, total), whole),
        ),
        out_shape=jax.ShapeDtypeStruct((rows, total), dtype),
        compiler_params=pltpu.CompilerParams(vmem_limit_bytes=60 << 20),
        name="hop",
    )(place.reshape(1), *arrivals, *own, *waits)


def sum_kernel(*refs):
    refs[-1][...] = tree_sum([ref[...] for ref in refs[:-1]]).astype(refs[-1].dtype)


def summed(parts, waits):
    shape = parts[0].shape
    return pl.pallas_call(
        held(sum_kernel, len(parts), len(waits)),
        grid=(1,),
        in_specs=[pl.BlockSpec(shape, lambda i: (0, 0))] * len(parts) + [anywhere] * len(waits),
        out_specs=pl.BlockSpec(shape, lambda i: (0, 0)),
        out_shape=jax.ShapeDtypeStruct(shape, parts[0].dtype),
        compiler_params=pltpu.CompilerParams(vmem_limit_bytes=60 << 20),
        name="summed",
    )(*parts, *waits)


def relay_kernel(count, mids, place_ref, *refs):
    parts, pieces = refs[:count], refs[count : 2 * count]
    mid_refs = refs[2 * count : 2 * count + mids]
    up_ref, normed_ref, sum_ref, *out_refs = refs[2 * count + mids :]
    mid_ref = out_refs.pop()
    sum_ref[...] = tree_sum([ref[...] for ref in parts]).astype(low)
    mid = mid_refs[0][...]
    for ref in mid_refs[1:]:
        mid = mid + ref[...]
    mid = mid.astype(low)
    mid_ref[...] = mid
    query_in = contract_leading(mid, normed_ref[...]).astype(low)
    rank, width = query_in.shape
    tokens, cols = pieces[0].shape
    group = up_ref.shape[1] // count
    for k, (ref, out_ref) in enumerate(zip(pieces, out_refs)):
        out_ref[:tokens] = ref[...]
        at = tokens
        for i in range(0, group, cols):
            start = pl.multiple_of(place_ref[k] * group + i, cols)
            out_ref[at : at + rank] = up_ref[:, pl.ds(start, cols)]
            at += rank
        for i in range(0, width, cols):
            out_ref[at : at + rank] = query_in[:, i : i + cols]
            at += rank


def relay(parts, pieces, mids, up, normed, waits):
    count, rank = len(parts), up.shape[0]
    tokens, cols = pieces[0].shape
    rows = tokens + rank * (up.shape[1] // count + normed.shape[1]) // cols
    places = jnp.stack([origin(0)] + [origin(count - k) for k in range(1, count)])
    inputs = (*parts, *pieces, *mids, up, normed)

    def whole(shape):
        return pl.BlockSpec(shape, lambda i, p: (0, 0))

    out = pl.pallas_call(
        held(functools.partial(relay_kernel, count, len(mids)), 1 + len(inputs), len(waits)),
        grid_spec=pltpu.PrefetchScalarGridSpec(
            num_scalar_prefetch=1,
            grid=(1,),
            in_specs=[whole(a.shape) for a in inputs] + [anywhere] * len(waits),
            out_specs=[whole(parts[0].shape)] + [whole((rows, cols))] * count + [whole((tokens, rank))],
        ),
        out_shape=[jax.ShapeDtypeStruct(parts[0].shape, low)]
        + [jax.ShapeDtypeStruct((rows, cols), low)] * count
        + [jax.ShapeDtypeStruct((tokens, rank), low)],
        compiler_params=pltpu.CompilerParams(vmem_limit_bytes=60 << 20),
        name="relay",
    )(places, *inputs, *waits)
    return out[0], out[1:-1], out[-1]


def head_forward(proj, gain, cos, sin):
    inv = lax.rsqrt(jnp.mean(proj * proj, axis=-1, keepdims=True) + norm_eps)
    scaled = proj * inv * gain
    return scaled * cos + pltpu.roll(scaled, HEAD_WIDTH // 2, 1) * sin, inv


def attend_kernel(share, proj_ref, cos_ref, sin_ref, gain_ref, bias_ref, key_ref, value_ref,
                  out_ref, lse_ref, value_t):
    @pl.when(lax.rem(pl.program_id(0), share) == 0)
    def _():
        value_t[...] = value_ref[...].T

    query, _ = head_forward(proj_ref[...], gain_ref[...], cos_ref[...], sin_ref[...])
    scores = contract_last(key_ref[...], query.astype(low)) * score_scale + bias_ref[...]
    top = jnp.max(scores, axis=0, keepdims=True)
    probs = jnp.exp(scores - top)
    total = jnp.sum(probs, axis=0, keepdims=True)
    mixed = product(value_t[...], probs.astype(low)) / total
    out_ref[...] = mixed.T.astype(low)
    lse_ref[0] = top + jnp.log(total)


def attend_back_kernel(share, pieces, extras, place_ref, proj_ref, cos_ref, sin_ref, gain_ref, bias_ref, key_ref, value_ref,
                       lse_ref, grad_ref, middle_ref, raise_ref, *refs):
    extra_refs, refs = refs[:extras], refs[extras:]
    out_ref, up_ref, *kv_refs = refs[: 2 + pieces]
    mid_ref, key_t, key_sum, value_sum = refs[2 + pieces :]

    @pl.when(pl.program_id(0) == 0)
    def _():
        mid_ref[...] = jnp.zeros_like(mid_ref)

    @pl.when(lax.rem(pl.program_id(0), share) == 0)
    def _():
        key_t[...] = key_ref[...].T
        key_sum[...] = jnp.zeros_like(key_sum)
        value_sum[...] = jnp.zeros_like(value_sum)

    proj, gain, cos, sin = proj_ref[...], gain_ref[...], cos_ref[...], sin_ref[...]
    query, inv = head_forward(proj, gain, cos, sin)
    query = query.astype(low)
    grad = grad_ref[...]
    scores = contract_last(key_ref[...], query) * score_scale + bias_ref[...]
    probs = jnp.exp(scores - lse_ref[0])
    probs_grad = contract_last(value_ref[...], grad)
    delta = jnp.sum(probs * probs_grad, axis=0, keepdims=True)
    scores_grad = (probs * (probs_grad - delta)).astype(low)
    value_sum[...] += product(probs.astype(low), grad)
    key_sum[...] += product(scores_grad, query)
    rotated = product(key_t[...], scores_grad).T * score_scale
    scaled = rotated * cos + pltpu.roll(rotated * sin, HEAD_WIDTH // 2, 1)
    scaled = scaled * gain
    slope = jnp.mean(scaled * proj, axis=-1, keepdims=True)
    proj_grad = (inv * scaled - proj * (inv * inv * inv * slope)).astype(low)
    out_ref[...] = proj_grad
    up_ref[...] = contract_leading(middle_ref[...], proj_grad).astype(low)
    mid_ref[...] += contract_last(proj_grad, raise_ref[...])

    @pl.when(lax.rem(pl.program_id(0), share) == share - 1)
    def _():
        for k, ref in enumerate(kv_refs):
            rows = proj_ref.shape[0]
            span = pl.ds(pl.multiple_of(place_ref[k] * rows, rows), rows)
            ref[:rows, :HEAD_WIDTH] = (key_sum[span, :] * score_scale).astype(low)
            ref[:rows, HEAD_WIDTH:] = value_sum[span, :].astype(low)
            if extras:
                common, mine = extra_refs
                more = mine.shape[0] // pieces
                ref[rows : rows + common.shape[0], :] = common[...]
                ref[rows + common.shape[0] :, :] = mine[pl.ds(pl.multiple_of(place_ref[k] * more, more), more), :]


def head_specs(tokens, length, first, share, kv_total):
    def head(h):
        return (0, first + h)

    def fixed(h):
        return (0, 0)

    return [
        pl.BlockSpec((tokens, HEAD_WIDTH), head),
        pl.BlockSpec((tokens, HEAD_WIDTH), fixed),
        pl.BlockSpec((tokens, HEAD_WIDTH), fixed),
        pl.BlockSpec((1, HEAD_WIDTH), fixed),
        pl.BlockSpec((length, tokens), fixed),
        pl.BlockSpec((length, HEAD_WIDTH), lambda h: (0, (first + h) // share)),
        pl.BlockSpec((length, HEAD_WIDTH), lambda h: (0, kv_total + (first + h) // share)),
    ]


def attend_cost(products, tokens, length, heads):
    return pl.CostEstimate(
        flops=4 * products * tokens * length * heads * HEAD_WIDTH,
        bytes_accessed=8 * tokens * heads * HEAD_WIDTH,
        transcendentals=tokens * length * heads,
    )


def attend(proj, cos, sin, gain, bias, keys_values):
    tokens, cols = proj.shape
    length, heads = keys_values.shape[0], cols // HEAD_WIDTH
    kv_total = keys_values.shape[1] // (2 * HEAD_WIDTH)
    share = heads // kv_total
    return pl.pallas_call(
        functools.partial(attend_kernel, share),
        grid=(heads,),
        in_specs=head_specs(tokens, length, 0, share, kv_total),
        out_specs=[
            pl.BlockSpec((tokens, HEAD_WIDTH), lambda h: (0, h)),
            pl.BlockSpec((1, 1, tokens), lambda h: (h, 0, 0)),
        ],
        scratch_shapes=[pltpu.VMEM((HEAD_WIDTH, length), low)],
        out_shape=[
            jax.ShapeDtypeStruct((tokens, cols), low),
            jax.ShapeDtypeStruct((heads, 1, tokens), wide),
        ],
        compiler_params=pltpu.CompilerParams(vmem_limit_bytes=60 << 20),
        cost_estimate=attend_cost(3, tokens, length, heads),
        name="attend",
    )(proj, cos, sin, gain, bias, keys_values, keys_values)


def attend_back(first, heads, kv_span, proj, cos, sin, gain, bias, keys_values, lse, grad, middle, raised,
                extras, filled, waits):
    tokens, length = proj.shape[0], keys_values.shape[0]
    rank = middle.shape[1]
    total = proj.shape[1] // HEAD_WIDTH
    kv_total = keys_values.shape[1] // (2 * HEAD_WIDTH)
    share, count = total // kv_total, length // tokens
    places = jnp.stack([origin(0)] + [origin(count - k) for k in range(1, count)])
    rows = tokens + (extras[0].shape[0] + extras[1].shape[0] // count if extras else 0)

    def with_place(spec):
        return pl.BlockSpec(spec.block_shape, lambda h, p: spec.index_map(h))

    def head(h, p):
        return (0, first + h)

    def kv_head(h, p):
        return (0, (first + h) // share - kv_span[0])

    return pl.pallas_call(
        held(
            functools.partial(attend_back_kernel, share, count, len(extras)),
            12 + len(extras),
            len(filled) + len(waits),
        ),
        grid_spec=pltpu.PrefetchScalarGridSpec(
            num_scalar_prefetch=1,
            grid=(heads,),
            in_specs=[with_place(spec) for spec in head_specs(tokens, length, first, share, kv_total)]
            + [
                pl.BlockSpec((1, 1, tokens), lambda h, p: (first + h, 0, 0)),
                pl.BlockSpec((tokens, HEAD_WIDTH), head),
                pl.BlockSpec((tokens, rank), lambda h, p: (0, 0)),
                pl.BlockSpec((rank, HEAD_WIDTH), head),
                *[pl.BlockSpec((a.shape[0], 2 * HEAD_WIDTH), kv_head) for a in extras],
                *[anywhere] * (len(filled) + len(waits)),
            ],
            out_specs=[
                pl.BlockSpec((tokens, HEAD_WIDTH), head),
                pl.BlockSpec((rank, HEAD_WIDTH), head),
                *[pl.BlockSpec((rows, 2 * HEAD_WIDTH), kv_head)] * count,
                pl.BlockSpec((tokens, rank), lambda h, p: (0, 0)),
            ],
            scratch_shapes=[
                pltpu.VMEM((HEAD_WIDTH, length), low),
                pltpu.VMEM((length, HEAD_WIDTH), wide),
                pltpu.VMEM((length, HEAD_WIDTH), wide),
            ],
        ),
        out_shape=[
            jax.ShapeDtypeStruct(proj.shape, low),
            jax.ShapeDtypeStruct((rank, proj.shape[1]), low),
            *[jax.ShapeDtypeStruct((rows, (kv_span[1] - kv_span[0]) * 2 * HEAD_WIDTH), low)] * count,
            jax.ShapeDtypeStruct((tokens, rank), wide),
        ],
        input_output_aliases={12 + len(extras) + i: i for i in range(len(filled))},
        compiler_params=pltpu.CompilerParams(vmem_limit_bytes=60 << 20),
        cost_estimate=pl.CostEstimate(flops=0, bytes_accessed=0, transcendentals=0),
        name="attend_back",
    )(places, proj, cos, sin, gain, bias, keys_values, keys_values, lse, grad, middle, raised,
      *extras, *filled, *waits)


def experts_kernel(place_ref, normed_ref, back_ref, weight_ref, gate_ref, up_ref, down_ref,
                   post_ref, out_ref, slice_ref, out_sum):
    e = pl.program_id(0)
    width = normed_ref.shape[1]

    @pl.when(e == 0)
    def _():
        post_ref[...] = jnp.zeros_like(post_ref)
        out_sum[...] = jnp.zeros_like(out_sum)

    normed = normed_ref[...]
    gate = product(normed, gate_ref[0])
    up = product(normed, up_ref[0])
    back = back_ref[...]
    weights = weight_ref[...]
    lane = lax.broadcasted_iota(jnp.int32, weights.shape, 1)
    weight = jnp.sum(jnp.where(lane == e, weights, 0.0), axis=1, keepdims=True)
    sig = jax.nn.sigmoid(gate)
    act = gate * sig
    inner = act * up
    lane = lax.broadcasted_iota(jnp.int32, (normed.shape[0], HEAD_WIDTH), 1)
    gate_sum = jnp.sum(inner * back, axis=1, keepdims=True)
    post_ref[:, width:] += jnp.where(lane == place_ref[1] + e, gate_sum, 0.0)
    back = back * weight
    gate_grad = (back * up * (sig + act * (1.0 - sig))).astype(low)
    up_grad = (back * act).astype(low)
    out_sum[...] += product((inner * weight).astype(low), down_ref[...])
    post_ref[:, :width] += contract_last(gate_grad, gate_ref[0]) + contract_last(up_grad, up_ref[0])

    @pl.when(e == pl.num_programs(0) - 1)
    def _():
        out_ref[...] = out_sum[...].astype(low)
        cols = slice_ref.shape[1]
        start = pl.multiple_of(place_ref[2] * cols, cols)
        slice_ref[...] = out_sum[:, pl.ds(start, cols)].astype(low)


def experts(place, tokens, slice_cols, normed, back, weights, gate_up, down, filled, waits):
    waits = (*filled, *waits)
    width = normed.shape[1]
    count, inner_width = gate_up.shape[0], gate_up.shape[2] // 2
    return pl.pallas_call(
        held(experts_kernel, 7, len(waits)),
        grid_spec=pltpu.PrefetchScalarGridSpec(
            num_scalar_prefetch=1,
            grid=(count,),
            in_specs=[
                pl.BlockSpec((tokens, width), lambda e, p: (p[0], 0)),
                pl.BlockSpec((tokens, inner_width), lambda e, p: (p[0], e)),
                pl.BlockSpec((tokens, count), lambda e, p: (p[0], 0)),
                pl.BlockSpec((1, width, inner_width), lambda e, p: (e, 0, 0)),
                pl.BlockSpec((1, width, inner_width), lambda e, p: (e, 0, 1)),
                pl.BlockSpec((inner_width, width), lambda e, p: (e, 0)),
                *[anywhere] * len(waits),
            ],
            out_specs=[
                pl.BlockSpec((tokens, width + HEAD_WIDTH), lambda e, p: (0, 0)),
                pl.BlockSpec((tokens, width), lambda e, p: (p[0], 0)),
                pl.BlockSpec((tokens, slice_cols), lambda e, p: (p[0], 0)),
            ],
            scratch_shapes=[pltpu.VMEM((tokens, width), wide)],
        ),
        out_shape=[
            jax.ShapeDtypeStruct((tokens, width + HEAD_WIDTH), wide),
            jax.ShapeDtypeStruct(normed.shape, low),
            jax.ShapeDtypeStruct((normed.shape[0], slice_cols), low),
        ],
        input_output_aliases={7 + i: 1 + i for i in range(len(filled))},
        compiler_params=pltpu.CompilerParams(vmem_limit_bytes=60 << 20),
        cost_estimate=pl.CostEstimate(
            flops=10 * tokens * width * count * inner_width,
            bytes_accessed=6 * width * count * inner_width,
            transcendentals=tokens * count * inner_width,
        ),
        name="experts",
    )(jnp.stack(place), normed, back, weights, gate_up, gate_up, down, *waits)


def settle_kernel(arrived_ref, post_ref, probs_ref, router_ref, resid_ref, gain_ref, cot_ref, up_ref,
                  branch_ref, middle_ref):
    width = resid_ref.shape[1]
    gate_grad = arrived_ref[:, width:].astype(wide) + post_ref[:, width:]
    probs = probs_ref[...]
    logits_grad = probs * (gate_grad - jnp.sum(probs * gate_grad, axis=1, keepdims=True))
    grad = arrived_ref[:, :width].astype(wide) + post_ref[:, :width]
    grad = (grad + product(logits_grad.astype(low), router_ref[...])) * gain_ref[...]
    resid = resid_ref[...]
    inv = lax.rsqrt(jnp.mean(resid * resid, axis=1, keepdims=True) + norm_eps)
    slope = jnp.mean(grad * resid, axis=1, keepdims=True)
    grad = cot_ref[...].astype(wide) + inv * grad - resid * (inv * inv * inv * slope)
    branch = grad.astype(low)
    branch_ref[...] = branch
    middle_ref[...] = contract_last(branch, up_ref[...]).astype(low)


def settle(arrived, post, probs, router, resid, gain, cot, up):
    tokens, width = resid.shape
    rank = up.shape[0]
    block = min(tokens, 64)
    lanes = arrived.shape[1] - width

    def rows(cols):
        return pl.BlockSpec((block, cols), lambda i: (i, 0))

    def whole(*shape):
        return pl.BlockSpec(shape, lambda i: (0, 0))

    return pl.pallas_call(
        settle_kernel,
        grid=(tokens // block,),
        in_specs=[
            rows(width + lanes),
            rows(width + lanes),
            rows(lanes),
            whole(lanes, width),
            rows(width),
            whole(1, width),
            rows(width),
            whole(rank, width),
        ],
        out_specs=[rows(width), rows(rank)],
        out_shape=[
            jax.ShapeDtypeStruct((tokens, width), low),
            jax.ShapeDtypeStruct((tokens, rank), low),
        ],
        compiler_params=pltpu.CompilerParams(vmem_limit_bytes=60 << 20),
        cost_estimate=pl.CostEstimate(flops=0, bytes_accessed=0, transcendentals=0),
        name="settle",
    )(arrived, post, probs, router, resid, gain, cot, up)


def update_kernel(rates, rank, row_width, slot_ref, place_ref, square_ref, head_ref, last_ref, *refs):
    size = 3 * len(rates)
    state, norm_ref, outs = refs[:size], refs[size], refs[size + 1 : 2 * size + 1]
    head_sum, last_sum, factor_ref = refs[2 * size + 1 :]
    now = pl.program_id(0)
    across_rows = rank * last_ref.shape[2] // head_ref.shape[2]
    in_start = head_ref.shape[1] - across_rows

    @pl.when(now == 0)
    def _():
        head_sum[...] = jnp.zeros_like(head_sum)
        last_sum[...] = jnp.zeros_like(last_sum)

        def tree(t, carry):
            at = slot_ref[t]
            head_sum[at] += head_ref[t].astype(wide)
            last_sum[at] += last_ref[t].astype(wide)
            return carry

        lax.fori_loop(0, head_ref.shape[0], tree, 0)

        def square(s, carry):
            for part in (head_sum[s, :across_rows], head_sum[s, in_start:], last_sum[s]):
                part = jnp.sum(part * part, axis=0, keepdims=True)
                carry = carry + jnp.sum(part, axis=1, keepdims=True)
            return carry

        norm = jnp.sqrt(lax.fori_loop(0, head_sum.shape[0], square, square_ref[...]))
        norm_ref[...] = norm
        factor_ref[...] = jnp.minimum(1.0, clip_limit / (norm + 1e-06))

    chunk = pl.multiple_of(rank * place_ref[0], rank)
    inside = pl.ds(pl.multiple_of(place_ref[1], HEAD_WIDTH), row_width)
    across = pl.ds(pl.multiple_of(place_ref[2], HEAD_WIDTH), row_width)

    def side_by_side(start, end):
        return jnp.concatenate([head_sum[now, i : i + rank] for i in range(start, end, rank)], axis=1)

    down_end = (across_rows + in_start) // 2
    kv = last_sum[now, 2 * rank :, :]
    kv_cols = state[-1].shape[2]
    grads = (
        side_by_side(down_end, in_start),
        side_by_side(across_rows, down_end),
        head_sum[now, pl.ds(chunk, rank), inside],
        jnp.concatenate(
            [head_sum[now, pl.ds(in_start + chunk, rank), inside], last_sum[now, : 2 * rank, across]], axis=0
        ),
        jnp.concatenate([kv[:, i : i + kv_cols] for i in range(0, kv.shape[1], kv_cols)], axis=0),
    )
    factor = factor_ref[...]
    for i, (grad, rate) in enumerate(zip(grads, rates)):
        weight, first, second = (ref[0] for ref in state[3 * i : 3 * i + 3])
        new = moment_update(weight, first, second, grad * factor, rate)
        for ref, value in zip(outs[3 * i : 3 * i + 3], new):
            ref[0] = value


def update(slots, place, square, head_trees, last_trees, states, rates, rank, row_width):
    state = [array for triple in states for array in triple]
    adapters = state[0].shape[0]

    def all_of(array):
        return pl.BlockSpec(array.shape, lambda s: (0,) * array.ndim)

    def one_of(array):
        return pl.BlockSpec((1, *array.shape[1:]), lambda s: (s, 0, 0))

    out = pl.pallas_call(
        functools.partial(update_kernel, tuple(rates), rank, row_width),
        grid=(adapters,),
        in_specs=[pl.BlockSpec(memory_space=pltpu.SMEM)] * 2
        + [all_of(a) for a in (square, head_trees, last_trees)]
        + [one_of(a) for a in state],
        out_specs=[all_of(square)] + [one_of(a) for a in state],
        out_shape=[jax.ShapeDtypeStruct((1, 1), wide)]
        + [jax.ShapeDtypeStruct(a.shape, wide) for a in state],
        scratch_shapes=[
            pltpu.VMEM((adapters, *head_trees.shape[1:]), wide),
            pltpu.VMEM((adapters, *last_trees.shape[1:]), wide),
            pltpu.VMEM((1, 1), wide),
        ],
        compiler_params=pltpu.CompilerParams(vmem_limit_bytes=60 << 20),
        name="update",
    )(slots, place, square, head_trees, last_trees, *state)
    return out[0], [out[1 + 3 * i : 4 + 3 * i] for i in range(len(states))]


def tree_layout(lengths, parents, token_count, first, count):
    nodes = lengths.shape[0]
    node_ids = jnp.arange(nodes, dtype=jnp.int32)
    node_ends = jnp.cumsum(lengths, dtype=jnp.int32)
    node_starts = node_ends - lengths
    parent_hot = parents[:, None] == node_ids[None, :]
    eye = node_ids[:, None] == node_ids[None, :]
    grand_hot = jnp.any(parent_hot[:, :, None] & parent_hot[None, :, :], axis=1)
    ancestor = eye | parent_hot | grand_hot
    before = jnp.sum(jnp.where(ancestor & ~eye, lengths[None, :], 0), axis=1, dtype=jnp.int32)

    def hot_of(tokens):
        return (tokens[:, None] >= node_starts[None, :]) & (tokens[:, None] < node_ends[None, :])

    keys = jnp.arange(token_count, dtype=jnp.int32)
    queries = first + jnp.arange(count, dtype=jnp.int32)
    query_hot = hot_of(queries)
    positions = queries + jnp.sum(
        jnp.where(query_hot, (before - node_starts)[None, :], 0), axis=1, dtype=jnp.int32
    )
    reach = product(query_hot.astype(low), ancestor.astype(low)).astype(low)
    reachable = contract_last(hot_of(keys).astype(low), reach) > 0.5
    allowed = reachable & (keys[:, None] <= queries[None, :])
    return positions, jnp.where(allowed, 0.0, masked_score)


def shards(
    inputs,
    cotangent,
    attention_norm_gain,
    expert_norm_gain,
    query_norm_gain,
    key_norm_gain,
    frozen_query_weight,
    frozen_key_weight,
    frozen_value_weight,
    frozen_output_weight,
    frozen_router_weight,
    expert_gate_up_weight,
    expert_down_weight,
    adapter_input_down,
    adapter_query_up,
    adapter_key_value_up,
    adapter_output_down,
    adapter_output_up,
    input_first_moment,
    input_second_moment,
    query_first_moment,
    query_second_moment,
    key_value_first_moment,
    key_value_second_moment,
    output_down_first_moment,
    output_down_second_moment,
    output_up_first_moment,
    output_up_second_moment,
    routes,
    tree_adapter_index,
    tree_node_length,
    parents,
):
    col_count = lax.axis_size("col")
    row_count = lax.axis_size("row")
    col_index = lax.axis_index("col")
    row_index = lax.axis_index("row")
    length, col_width = inputs.shape
    width = col_width * col_count
    tokens = length // col_count
    first_token = col_index * tokens
    row_width = frozen_key_weight.shape[0]
    group_cols = frozen_query_weight.shape[1]
    kv_total = frozen_key_weight.shape[1] // HEAD_WIDTH
    kv_cols = kv_total * HEAD_WIDTH
    rank = adapter_query_up.shape[1]
    adapters = adapter_input_down.shape[0]
    local_experts = expert_gate_up_weight.shape[0]
    expert_total = frozen_router_weight.shape[1]
    inner_width = expert_down_weight.shape[1]
    slot = tree_adapter_index[0]

    def gather_rows(values, axis):
        return lax.all_gather(values, "row", axis=axis, tiled=True)

    local_inner = local_experts * inner_width
    first = gather_rows(
        jnp.concatenate(
            [
                expert_down_weight.reshape(local_inner, row_width),
                adapter_input_down.transpose(0, 2, 1).reshape(-1, row_width).astype(low),
                adapter_output_up.transpose(0, 2, 1).reshape(-1, row_width).astype(low),
                frozen_router_weight.T,
                jnp.broadcast_to(slot.astype(low), (16, row_width)),
                frozen_key_weight.T,
                frozen_value_weight.T,
            ]
        ),
        1,
    )
    in_start = local_inner
    up_start = in_start + adapters * 3 * rank
    router_start = up_start + adapters * rank
    slot_start = router_start + expert_total
    kv_start = slot_start + 16
    down_input = lax.dynamic_slice_in_dim(first, in_start + slot * 3 * rank, 3 * rank, 0)
    up_output = lax.dynamic_slice_in_dim(first, up_start + slot * rank, rank, 0)
    router = first[router_start:slot_start]
    slots = first[slot_start, ::row_width].astype(jnp.int32)
    key_value_weight = first[kv_start:]
    query_weight = gather_rows(in_order(ring_gather(frozen_query_weight), 1), 0)
    out_weight = gather_rows(in_order(ring_gather(frozen_output_weight), 0), 1)
    gate_up_weight = gather_rows(expert_gate_up_weight, 1)
    head_adapters = in_order(
        ring_gather(
            jnp.concatenate([adapter_query_up[slot], adapter_output_down[slot].T]).astype(low)
        ),
        1,
    )
    query_raise = head_adapters[:rank]
    down_output = head_adapters[rank:]
    key_value_raise = adapter_key_value_up[slot].astype(low)

    pieces = exchange(lambda c: lax.dynamic_slice_in_dim(inputs, c * tokens, tokens, 0))
    hidden_input = in_order(pieces, 1).astype(wide)
    cot_full = in_order(ring_gather(cotangent), 1)
    cot_own = lax.dynamic_slice_in_dim(cot_full, first_token, tokens, 0)
    positions, bias = tree_layout(tree_node_length[0], parents[0], length, first_token, tokens)

    def norm_in(values):
        return rms_norm(values, attention_norm_gain)

    normalized, norm_in_back = jax.vjp(norm_in, hidden_input)
    normalized = normalized.astype(low)
    middle = contract_last(normalized, down_input).astype(low)
    half = HEAD_WIDTH // 2
    frequency = rope_base ** (-jnp.arange(half, dtype=wide) / half)
    angles = positions.astype(wide)[:, None] * frequency[None, :]
    cos = jnp.concatenate([jnp.cos(angles)] * 2, axis=1)
    sin = jnp.concatenate([-jnp.sin(angles), jnp.sin(angles)], axis=1)

    def shape_keys(proj):
        parts = []
        for head in range(kv_total):
            scaled = rms_norm(proj[:, head * HEAD_WIDTH : (head + 1) * HEAD_WIDTH], key_norm_gain)
            turned = jnp.concatenate([scaled[:, half:], scaled[:, :half]], axis=1)
            parts.append(scaled * cos + turned * sin)
        return jnp.concatenate(parts, axis=1)

    key_value_proj = contract_last(normalized, key_value_weight)
    key_proj = key_value_proj[:, :kv_cols] + product(middle[:, rank : 2 * rank], key_value_raise[0])
    value_proj = key_value_proj[:, kv_cols:] + product(middle[:, 2 * rank :], key_value_raise[1])
    key_rot, keys_back = jax.vjp(shape_keys, key_proj)
    keys_values = in_order(
        ring_gather(jnp.concatenate([key_rot.astype(low), value_proj.astype(low)], axis=1)), 0
    )
    query_gain = query_norm_gain[None, :]
    proj = project(normalized, query_weight, (middle[:, :rank], query_raise), False, wide)
    heads, totals = attend(proj, cos, sin, query_gain, bias, keys_values)
    inner_back = contract_last(cot_full, first[:local_inner])
    middle_output = contract_last(heads, down_output).astype(low)
    resid = hidden_input + project(
        heads, out_weight, (middle_output, up_output), False, wide, (inner_back,)
    )

    resid_full = in_order(ring_gather(resid.astype(low)), 0)
    normed_post = rms_norm(resid_full.astype(wide), expert_norm_gain).astype(low)
    logits = contract_last(normed_post, router)
    expert_ids = jnp.arange(expert_total, dtype=jnp.int32)
    chosen = jnp.any(routes[:, :, None] == expert_ids[None, None, :], axis=1)
    shifted = logits - jnp.max(jnp.where(chosen, logits, -jnp.inf), axis=1, keepdims=True)
    raised = jnp.where(chosen, jnp.exp(jnp.where(chosen, shifted, 0.0)), 0.0)
    gate_probs = raised / jnp.sum(raised, axis=1, keepdims=True)
    local_probs = lax.dynamic_slice_in_dim(gate_probs, col_index * local_experts, local_experts, 1)
    own_probs = jnp.pad(
        lax.dynamic_slice_in_dim(gate_probs, first_token, tokens, 0),
        ((0, 0), (0, HEAD_WIDTH - expert_total)),
    )
    router_rows = jnp.pad(router, ((0, HEAD_WIDTH - expert_total), (0, 0)))
    filled, arrived, sent = (), None, ()
    for k in range(col_count):
        post, *filled = experts(
            (origin(k + 1), col_index * local_experts, origin(1)),
            tokens,
            col_width,
            normed_post,
            inner_back,
            local_probs,
            gate_up_weight,
            first,
            filled,
            sent if k < col_count - 1 else (*sent, own_probs, router_rows, cot_own),
        )
        if k < col_count - 1:
            sent = ((post if k == 0 else arrived.astype(wide) + post).astype(low),)
            arrived = shift(sent[0], 1)

    mixture, mixture_sent = filled

    def mixture_hop(k, arrived, dtype, *waits):
        return hop(origin(k), arrived, (mixture,), (length, col_width), dtype, waits)

    branch_grad, mid_out_grad = settle(
        arrived, post, own_probs, router_rows, resid, expert_norm_gain[None, :], cot_own, up_output
    )
    heads_grad = project(branch_grad, out_weight, (mid_out_grad, down_output), True, low)

    def folded(part, cols):
        return jnp.concatenate([part[:, i : i + cols] for i in range(0, part.shape[1], cols)])

    query_middle = middle[:, :rank]
    half_cols = kv_cols
    down_portion = folded(contract_leading(mid_out_grad, heads).astype(low), half_cols)
    up_portion = folded(contract_leading(middle_output, branch_grad).astype(low), half_cols)
    head_count = proj.shape[1] // HEAD_WIDTH
    quarter, half_kv = head_count // 4, kv_total // 2

    def heads_back(first, count, kv_first, extras, filled, waits):
        return attend_back(
            first * quarter,
            count * quarter,
            (kv_first, kv_first + half_kv),
            proj,
            cos,
            sin,
            query_gain,
            bias,
            keys_values,
            totals,
            heads_grad,
            query_middle,
            query_raise,
            extras,
            filled,
            waits,
        )

    def sent_on(pieces):
        return [pieces[0]] + [shift(pieces[k], k) for k in range(1, col_count)]

    extras = (up_portion, down_portion)
    *filled, mid_a = heads_back(0, 1, 0, extras, (), ())
    mixture_sent = mixture_hop(2, shift(mixture_sent, 1), low, filled[0])
    mixture_arrived = shift(mixture_sent, 1)
    query_grad, query_portion, *pieces, mid_b = heads_back(1, 1, 0, extras, filled, (mixture_sent,))
    pieces = sent_on(pieces)
    query_grad, query_portion, *leaving, mid_c = heads_back(
        2, 2, half_kv, (), (query_grad, query_portion), ()
    )
    first_sum, leaving, mid_query_grad = relay(
        pieces, leaving, (mid_a, mid_b, mid_c), query_portion, normalized, (mixture_arrived,)
    )
    pieces = sent_on(leaving)
    normed_query_grad = project(query_grad, query_weight, (), True, wide, (first_sum,))
    second_sum = summed(pieces, (normed_query_grad,))
    kv_own = jnp.concatenate([first_sum[:tokens], second_sum[:tokens]], axis=1).astype(wide)
    head_sum = jnp.concatenate([first_sum[tokens:], second_sum[tokens:]])
    kv_split = [kv_own[:, i : i + HEAD_WIDTH] for i in range(0, 2 * kv_cols, HEAD_WIDTH)]
    key_grad = keys_back(jnp.concatenate(kv_split[0::2], axis=1))[0].astype(low)
    value_grad = jnp.concatenate(kv_split[1::2], axis=1).astype(low)
    kv_proj_grad = jnp.concatenate([key_grad, value_grad], axis=1)
    mid_kv_grad = jnp.concatenate(
        [
            contract_last(key_grad, key_value_raise[0]),
            contract_last(value_grad, key_value_raise[1]),
        ],
        axis=1,
    ).astype(low)

    kv_portion = jnp.concatenate(
        [
            contract_leading(middle[:, rank : 2 * rank], key_grad),
            contract_leading(middle[:, 2 * rank :], value_grad),
        ]
    )
    kv_rows = 2 * rank * kv_cols // width
    kv_portion = jnp.concatenate(
        [kv_portion[i : i + kv_rows] for i in range(0, 2 * rank, kv_rows)], axis=1
    )
    last_part = jnp.concatenate([contract_leading(mid_kv_grad, normalized), kv_portion]).astype(low)
    last_sum = tree_sum([last_part] + [shift(last_part, k) for k in range(1, col_count)]).astype(low)
    last_trees = lax.all_gather(last_sum, "row", axis=0)
    head_trees = lax.all_gather(head_sum, "row", axis=0)
    wait = nought(last_sum)
    slot_hot = slots[None, :] == wait + jnp.arange(adapters, dtype=jnp.int32)[:, None]
    slot_hot = slot_hot.astype(low)
    across_rows = rank * width // half_cols
    head_square = jnp.einsum(
        "st,tij->sij",
        slot_hot,
        head_trees[:, across_rows : head_sum.shape[0] - across_rows],
        preferred_element_type=wide,
    )
    head_square = jnp.full((1, HEAD_WIDTH), jnp.sum(head_square * head_square))
    step = 1
    while step < col_count:
        pairs = [(i, i ^ step) for i in range(col_count)]
        head_square = head_square + lax.ppermute(head_square, "col", pairs)
        step *= 2
    head_square = head_square[:, :1]

    normed_in_grad = (
        normed_query_grad
        + product(kv_proj_grad, key_value_weight)
        + product(jnp.concatenate([mid_query_grad, mid_kv_grad], axis=1), down_input)
    )
    input_grad_own = (branch_grad.astype(wide) + norm_in_back(normed_in_grad)[0]).astype(low)
    pieces = exchange(
        lambda c: lax.dynamic_slice_in_dim(input_grad_own, c * col_width + wait, col_width, 1)
    )
    input_grad = in_order(pieces, 0).astype(wide)
    waits = (head_square, *pieces[1:])
    for k in range(2, col_count - 1):
        mixture_sent = mixture_hop(k + 1, mixture_arrived, low, *waits)
        mixture_arrived, waits = shift(mixture_sent, 1), ()
    own_slice = lax.dynamic_slice_in_dim(mixture, col_index * col_width, col_width, 1)
    moe_slice = mixture_arrived.astype(wide) + own_slice.astype(wide)
    resid_slice = lax.dynamic_slice_in_dim(resid_full, col_index * col_width, col_width, 1)
    layer_output = resid_slice.astype(wide) + moe_slice

    def flip(array):
        return array.transpose(0, 2, 1)

    def rows_of(array):
        return array.reshape(adapters, 2 * rank, kv_cols)

    row_start = row_index * row_width
    place = jnp.stack([row_start // half_cols, lax.rem(row_start, half_cols), row_start])
    grad_norm, following = update(
        slots,
        place,
        head_square,
        head_trees,
        last_trees,
        (
            (adapter_query_up, query_first_moment, query_second_moment),
            tuple(map(flip, (adapter_output_down, output_down_first_moment, output_down_second_moment))),
            tuple(map(flip, (adapter_output_up, output_up_first_moment, output_up_second_moment))),
            tuple(map(flip, (adapter_input_down, input_first_moment, input_second_moment))),
            tuple(map(rows_of, (adapter_key_value_up, key_value_first_moment, key_value_second_moment))),
        ),
        (
            learning_rate_upper,
            learning_rate_output,
            learning_rate_upper,
            learning_rate_lower,
            learning_rate_upper,
        ),
        rank,
        row_width,
    )
    query_following, down_following, up_following, input_following, key_value_following = following
    return (
        layer_output,
        input_grad,
        grad_norm.reshape(()),
        *map(flip, input_following),
        *query_following,
        *(a.reshape(adapter_key_value_up.shape) for a in key_value_following),
        *map(flip, down_following),
        *map(flip, up_following),
        moe_slice,
    )


def solution(mesh):
    return jax.shard_map(
        shards,
        mesh=mesh,
        in_specs=(
            P("row", "col"),
            P("row", "col"),
            P(),
            P(),
            P(),
            P(),
            P("row", "col"),
            P("row", None),
            P("row", None),
            P("col", "row"),
            P("row", None),
            P("col", "row", None),
            P("col", None, "row"),
            P(None, "row", None),
            P(None, None, "col"),
            P(),
            P(None, "col", None),
            P(None, "row", None),
            P(None, "row", None),
            P(None, "row", None),
            P(None, None, "col"),
            P(None, None, "col"),
            P(),
            P(),
            P(None, "col", None),
            P(None, "col", None),
            P(None, "row", None),
            P(None, "row", None),
            P("row", None),
            P("row"),
            P("row", None),
            P("row", None),
        ),
        out_specs=(
            P("row", "col"),
            P("row", "col"),
            P(),
            P(None, "row", None),
            P(None, "row", None),
            P(None, "row", None),
            P(None, None, "col"),
            P(None, None, "col"),
            P(None, None, "col"),
            P(),
            P(),
            P(),
            P(None, "col", None),
            P(None, "col", None),
            P(None, "col", None),
            P(None, "row", None),
            P(None, "row", None),
            P(None, "row", None),
            P("row", "col"),
        ),
        check_vma=False,
    )
```
